256 devices in a mesh: dp: 32 (over x_lo, z, core), fsdp: 8 (over y, x_hi).
Axes of the slice: x: 4 (x_hi: 2, x_lo: 2; x = x_hi * 2 + x_lo), y: 4, z: 8, core: 2. Of those that a mesh axis runs over, the one named last changes fastest.
Arguments:
- patches: bfloat16 [256, 8, 48, 1152], P(('dp', 'fsdp')), may hold values from -6 to 6
- counts: int32 [256, 8], P(('dp', 'fsdp')), may hold values from 1 to 48, as said below
- owners: int32 [256, 8], P(('dp', 'fsdp')), may hold values from 0 to 7, as said below
- captions: bfloat16 [256, 8, 1152], P(('dp', 'fsdp')), may hold values from -6 to 6
- norm_gain: float32 [1152], replicated, may hold values from 0.25 to 1.75
- key_probe: bfloat16 [1152, 16], replicated, may hold values from -12 to 12
- value_weight: bfloat16 [1152, 1152], P('fsdp'), may hold values from -0.1875 to 0.1875
- logit_scale: float32 [1], replicated, may hold values from 5 to 20
- logit_bias: float32 [1], replicated, may hold values from -4 to -1
Outputs:
- loss_part: float32 [32, 8], P('dp', 'fsdp')
- row_grad: bfloat16 [256, 8, 48, 1152], P(('dp', 'fsdp'))
- text_grad: bfloat16 [256, 8, 1152], P(('dp', 'fsdp'))
- value_grad: bfloat16 [32, 1152, 1152], P('dp', 'fsdp')
- probe_grad: bfloat16 [32, 1152, 16], P('dp', 'fsdp')
- gain_grad: bfloat16 [32, 1152], P('dp', 'fsdp')
The draws below stay inside these ranges and needn't reach their ends.
Inputs may be any that keep to these rules, and one draw needn't show every extreme that they name: `counts`: each loader holds at least one image of exactly 48 rows. `owners`: each loader sends exactly 1 of its images to every device of its data rank.
All inputs are finite; a program needn't handle non-finite values.
Results may differ from the reference program's by a relative error of at most 0.02.
Values may be sent and summed in bfloat16 or wider, within the bound.
No kernel may reach another device: no remote copies, remote signals or barrier semaphores. Data moves between devices by JAX's collectives and lax.ppermute only.
A program may use at most 64 MiB of HBM per device.

```python
import math
import jax
import jax.numpy as jnp
from jax import lax

D = 1152
HEADS = 16
PATCHES = 48
PAIR_IMAGES = 1
SLOTS = 8
N_DP = 32
N_FSDP = 8
DEVICES = 256


def draw_counts(key, part):
    key = jax.random.fold_in(key, 3)
    first, second = jax.random.split(key)
    sizes_drawn = jax.random.randint(first, (DEVICES, SLOTS), 1, PATCHES + 1)
    full_at = jax.random.randint(second, (DEVICES, 1), 0, SLOTS)
    position = jnp.arange(SLOTS)[None, :]
    return jnp.where(position == full_at, PATCHES, sizes_drawn).astype(jnp.int32)


def draw_owners(key, part):
    key = jax.random.fold_in(key, 5)
    ranks = jnp.tile(jnp.arange(SLOTS, dtype=jnp.int32) % N_FSDP, (DEVICES, 1))
    return jax.random.permutation(key, ranks, axis=1, independent=True).astype(jnp.int32)


def draw_key_probe(key, part):
    key = jax.random.fold_in(key, 7)
    first = jax.random.fold_in(key, 0)
    base = jnp.clip(jax.random.normal(first, (D, HEADS), jnp.float32), -4.0, 4.0)
    return (base * 0.5).astype(jnp.bfloat16)


def steps_of(rng, dims, cuts, smallest, top_value):
    loudness, own = 1.0, jax.random.fold_in(rng, 6)
    for dim, shards_of in cuts:
        draws = jnp.exp(jax.random.uniform(jax.random.fold_in(own, dim), (shards_of,), jnp.float32, smallest / len(cuts), top_value / len(cuts)))
        loudness = loudness * jnp.repeat(draws, dims[dim] // shards_of).reshape([-1 if axis == dim else 1 for axis in range(len(dims))])
    return loudness


def normal_values(rng, shape, deviation, most, shards=(), kind=jnp.bfloat16):
    factor_of = steps_of(rng, shape, shards, -0.22, 0.18) if shards else 1.0
    values = jax.random.normal(rng, shape, jnp.float32) * deviation * factor_of
    return jnp.minimum(jnp.maximum(values, -most), most).astype(kind)


def setup_inputs(seed: int = 0) -> dict:
    splits = jax.random.split(jax.random.key(seed), 10)
    patches = normal_values(splits[0], (DEVICES, SLOTS, PATCHES, D), 1.0, 6.0, ((0, 256),))
    counts = draw_counts(jax.random.fold_in(splits[9], 71), 0)
    owners = draw_owners(jax.random.fold_in(splits[9], 71), 0)
    captions = normal_values(splits[3], (DEVICES, SLOTS, D), 1.0, 6.0, ((0, 256),))
    norm_gain = jnp.clip(1.0 + 0.15 * jax.random.normal(splits[4], (D,), jnp.float32), 0.25, 1.75)
    key_probe = draw_key_probe(jax.random.fold_in(splits[9], 71), 0)
    value_weight = normal_values(splits[6], (D, D), D ** -0.5, 0.1875, ((0, 8),))
    logit_scale = jnp.clip(jnp.exp(jax.random.uniform(splits[7], (1,), jnp.float32, math.log(5.0), math.log(20.0))), 5.0, 20.0)
    logit_bias = jnp.clip(jax.random.uniform(splits[8], (1,), jnp.float32, -4.0, -1.0), -4.0, -1.0)
    return dict(patches=patches, counts=counts, owners=owners, captions=captions, norm_gain=norm_gain, key_probe=key_probe, value_weight=value_weight, logit_scale=logit_scale, logit_bias=logit_bias)


epsilon = 1e-06

def pack_loader(loaded, sizes_in, targets):
    slot_count = targets.shape[0]
    position = jnp.arange(slot_count, dtype=jnp.int32)
    before = (targets[:, None] == targets[None, :]) & (position[None, :] < position[:, None])
    earlier = lax.optimization_barrier(jnp.sum(before.astype(jnp.int32), axis=1)).astype(jnp.int32)
    placed = (targets * PAIR_IMAGES + earlier).astype(jnp.int32)
    source = lax.optimization_barrier(jnp.sum(jnp.where(placed[None, :] == position[:, None], position[None, :], 0), axis=1)).astype(jnp.int32)
    return (jnp.take(loaded, source, axis=0), jnp.take(sizes_in, source, axis=0))

def encode(received, sizes_now, norm_gain, key_probe, value_weight):
    slot_count, patch_count, model_width = received.shape
    head_count = key_probe.shape[1]
    head_width = model_width // head_count
    flat_rows = received.reshape(slot_count * patch_count, model_width).astype(jnp.float32)
    row_mean = lax.optimization_barrier(jnp.mean(flat_rows, axis=-1, keepdims=True))
    centered = flat_rows - row_mean
    inv_std = lax.rsqrt(lax.optimization_barrier(jnp.mean(centered * centered, axis=-1, keepdims=True)) + epsilon)
    normed = centered * inv_std
    scaled_in = (normed * norm_gain).astype(jnp.bfloat16)
    scores = jnp.dot(scaled_in, key_probe, preferred_element_type=jnp.float32).reshape(slot_count, patch_count, head_count) / math.sqrt(head_width)
    valid_rows = jnp.arange(patch_count, dtype=jnp.int32)[None, :, None] < sizes_now[:, None, None]
    highest = lax.optimization_barrier(jnp.max(jnp.where(valid_rows, scores, -jnp.inf), axis=1, keepdims=True))
    raised = jnp.where(valid_rows, jnp.exp(scores - highest), 0.0)
    weights_f = raised / lax.optimization_barrier(jnp.sum(raised, axis=1, keepdims=True))
    weights_b = weights_f.astype(jnp.bfloat16)
    values = jnp.dot(scaled_in, value_weight, preferred_element_type=jnp.float32).astype(jnp.bfloat16)
    values = values.reshape(slot_count, patch_count, head_count, head_width)
    context = jnp.einsum('sph,sphe->she', weights_b.astype(jnp.float32), values.astype(jnp.float32)).reshape(slot_count, model_width)
    inv_norm = lax.rsqrt(lax.optimization_barrier(jnp.sum(context * context, axis=-1, keepdims=True)) + epsilon)
    unit_image = context * inv_norm
    return (normed, inv_std, scaled_in, weights_f, weights_b, values, unit_image, inv_norm)

def backward_device(received, sizes_now, d_image, norm_gain, key_probe, value_weight):
    normed, inv_std, scaled_in, weights_f, weights_b, values, unit_image, inv_norm = encode(received, sizes_now, norm_gain, key_probe, value_weight)
    slot_count, patch_count, head_count, head_width = values.shape
    model_width = head_count * head_width
    d_embed = (d_image - unit_image * lax.optimization_barrier(jnp.sum(d_image * unit_image, axis=-1, keepdims=True))) * inv_norm
    d_context = d_embed.astype(jnp.bfloat16).reshape(slot_count, head_count, head_width)
    d_weights = jnp.einsum('she,sphe->sph', d_context.astype(jnp.float32), values.astype(jnp.float32))
    d_values = (weights_b.astype(jnp.float32)[..., None] * d_context.astype(jnp.float32)[:, None]).astype(jnp.bfloat16)
    d_values = d_values.reshape(slot_count * patch_count, model_width)
    d_scores = (weights_f * (d_weights - lax.optimization_barrier(jnp.sum(weights_f * d_weights, axis=1, keepdims=True))) / math.sqrt(head_width)).astype(jnp.bfloat16)
    d_scores = d_scores.reshape(slot_count * patch_count, head_count)
    value_term = jnp.dot(scaled_in.T, d_values, preferred_element_type=jnp.float32)
    probe_term = jnp.dot(scaled_in.T, d_scores, preferred_element_type=jnp.float32)
    d_scaled = jnp.dot(d_values, value_weight.T, preferred_element_type=jnp.float32) + jnp.dot(d_scores, key_probe.T, preferred_element_type=jnp.float32)
    gain_term = lax.optimization_barrier(jnp.sum(d_scaled * normed, axis=0))
    grad_in = d_scaled * norm_gain
    row_grad = inv_std * (grad_in - lax.optimization_barrier(jnp.mean(grad_in, axis=-1, keepdims=True)) - normed * lax.optimization_barrier(jnp.mean(grad_in * normed, axis=-1, keepdims=True)))
    return (row_grad.astype(jnp.bfloat16).reshape(slot_count, patch_count, model_width), value_term.astype(jnp.bfloat16), probe_term.astype(jnp.bfloat16), gain_term.astype(jnp.bfloat16))

def reference(patches, counts, owners, captions, norm_gain, key_probe, value_weight, logit_scale, logit_bias):
    sent, sent_sizes = jax.vmap(pack_loader)(patches, counts, owners)
    received = sent.reshape(N_DP, N_FSDP, N_FSDP, PAIR_IMAGES, PATCHES, D).transpose(0, 2, 1, 3, 4, 5).reshape(DEVICES, SLOTS, PATCHES, D)
    sizes_now = sent_sizes.reshape(N_DP, N_FSDP, N_FSDP, PAIR_IMAGES).transpose(0, 2, 1, 3).reshape(DEVICES, SLOTS)

    def image_of(entries):
        return encode(entries[0], entries[1], norm_gain, key_probe, value_weight)[6].astype(jnp.bfloat16)
    images = lax.map(image_of, (received, sizes_now))
    caption_f = captions.astype(jnp.float32)
    caption_inv = lax.rsqrt(lax.optimization_barrier(jnp.sum(caption_f * caption_f, axis=-1, keepdims=True)) + epsilon)
    caption_unit = caption_f * caption_inv
    caption_b = caption_unit.astype(jnp.bfloat16)
    batch_size = DEVICES * SLOTS
    all_images = images.reshape(batch_size, D)
    all_captions = caption_b.reshape(batch_size, D)
    matched = jnp.eye(batch_size, dtype=jnp.float32)
    logits = logit_scale[0] * jnp.einsum('ad,bd->ab', all_images.astype(jnp.float32), all_captions.astype(jnp.float32)) + logit_bias[0]
    losses = jax.nn.softplus((1.0 - 2.0 * matched) * logits)
    coefficient = (logit_scale[0] * (jax.nn.sigmoid(logits) - matched)).astype(jnp.bfloat16)
    device_loss = lax.optimization_barrier(jnp.sum(losses.reshape(DEVICES, SLOTS * batch_size), axis=1)) / batch_size
    loss_part = device_loss.reshape(N_DP, N_FSDP)
    d_images = jnp.dot(coefficient, all_captions, preferred_element_type=jnp.float32).reshape(DEVICES, SLOTS, D)
    d_captions = jnp.dot(coefficient.T, all_images, preferred_element_type=jnp.float32).reshape(DEVICES, SLOTS, D)
    text_grad = ((d_captions - caption_unit * lax.optimization_barrier(jnp.sum(d_captions * caption_unit, axis=-1, keepdims=True))) * caption_inv).astype(jnp.bfloat16)

    def one_device(entries):
        return backward_device(entries[0], entries[1], entries[2], norm_gain, key_probe, value_weight)

    def one_rank(entries):
        rows_out, value_terms, probe_terms, gain_terms = lax.map(one_device, entries)
        return (rows_out, lax.optimization_barrier(jnp.sum(value_terms.astype(jnp.float32), axis=0)).astype(jnp.bfloat16), lax.optimization_barrier(jnp.sum(probe_terms.astype(jnp.float32), axis=0)).astype(jnp.bfloat16), lax.optimization_barrier(jnp.sum(gain_terms.astype(jnp.float32), axis=0)).astype(jnp.bfloat16))
    rank_rows, value_grad, probe_grad, gain_grad = lax.map(one_rank, (received.reshape(N_DP, N_FSDP, SLOTS, PATCHES, D), sizes_now.reshape(N_DP, N_FSDP, SLOTS), d_images.reshape(N_DP, N_FSDP, SLOTS, D)))
    row_grad = rank_rows.reshape(DEVICES, SLOTS, PATCHES, D)
    return (loss_part, row_grad, text_grad, value_grad, probe_grad, gain_grad)
```

```python
import math

import jax
import jax.numpy as jnp
from jax import lax
from jax.experimental import pallas as pl
from jax.experimental.pallas import tpu as pltpu
from jax.sharding import PartitionSpec as P

epsilon = 1e-06
F32 = jnp.float32
BF16 = jnp.bfloat16

VMEM_LIMIT = 40 * 1024 * 1024
SEND_ROWS = 80


def vspec():
    return pl.BlockSpec(memory_space=pltpu.VMEM)


def sspec():
    return pl.BlockSpec(memory_space=pltpu.SMEM)


def call(body, out_shapes, in_specs, flops, nbytes, scratch=(), name=None):
    return pl.pallas_call(
        body,
        out_shape=out_shapes,
        in_specs=in_specs,
        out_specs=[vspec() for _ in out_shapes],
        scratch_shapes=list(scratch),
        compiler_params=pltpu.CompilerParams(vmem_limit_bytes=VMEM_LIMIT),
        cost_estimate=pl.CostEstimate(flops=flops, bytes_accessed=nbytes, transcendentals=0),
        name=name,
    )


def nt_dot(a, b):
    return lax.dot_general(a, b, (((1,), (1,)), ((), ())), preferred_element_type=F32)


def tn_dot(a, b):
    return lax.dot_general(a, b, (((0,), (0,)), ((), ())), preferred_element_type=F32)


def head_mask(heads, width):
    head_width = width // heads
    low = lax.broadcasted_iota(jnp.int32, (heads, width), 0) * head_width
    column = lax.broadcasted_iota(jnp.int32, (heads, width), 1)
    return ((column >= low) & (column < low + head_width)).astype(F32)


def pool_body(owners, counts, x_ref, gain_ref, probe_ref, normed_ref, scaled_ref, inv_ref, w_ref, a_ref):
    slots, rows, width = x_ref.shape
    heads = probe_ref.shape[0]
    scale = 1.0 / math.sqrt(width // heads)
    gain = gain_ref[...]
    probe = probe_ref[...]
    for r in range(slots):
        source = jnp.int32(0)
        for k in range(slots):
            source = source + jnp.where(owners[k] == r, k, 0)
        x = x_ref[source].astype(F32)
        mean = jnp.sum(x, axis=-1, keepdims=True) * (1.0 / width)
        centered = x - mean
        var = jnp.sum(centered * centered, axis=-1, keepdims=True) * (1.0 / width)
        inv = lax.rsqrt(var + epsilon)
        normed = centered * inv
        scaled = (normed * gain).astype(BF16)
        scores = nt_dot(probe, scaled) * scale
        valid = lax.broadcasted_iota(jnp.int32, (heads, rows), 1) < counts[source]
        highest = jnp.max(jnp.where(valid, scores, -jnp.inf), axis=-1, keepdims=True)
        raised = jnp.where(valid, jnp.exp(scores - highest), 0.0)
        weights = raised / jnp.sum(raised, axis=-1, keepdims=True)
        normed_ref[r] = normed
        scaled_ref[r] = scaled
        inv_ref[r] = jnp.broadcast_to(inv, inv_ref.shape[1:])
        w_ref[r] = weights
        a_ref[r] = jnp.dot(weights.astype(BF16), scaled, preferred_element_type=F32).astype(BF16)


def image_body(place, mine_ref, other_ref, a_ref, sent_a_ref, full_ref, unit_ref, inv_ref, out_ref):
    shards, part_rows, width = mine_ref.shape
    slots, heads, _ = a_ref.shape
    shard_rows = width // shards

    def put(low_ref, high_ref):
        skip = 2 * part_rows - shard_rows
        for j in range(shards):
            full_ref[pl.ds(j * shard_rows, part_rows), :] = low_ref[j]
            full_ref[pl.ds(j * shard_rows + part_rows, shard_rows - part_rows), :] = high_ref[
                j, pl.ds(skip, part_rows - skip), :
            ]

    @pl.when(place[2] == 0)
    def _():
        put(mine_ref, other_ref)

    @pl.when(place[2] != 0)
    def _():
        put(other_ref, mine_ref)

    wide = jnp.dot(
        a_ref[...].reshape(slots * heads, width), full_ref[...], preferred_element_type=F32
    ).reshape(slots, heads, width)
    context = jnp.sum(wide * head_mask(heads, width)[None], axis=1)
    inv = lax.rsqrt(jnp.sum(context * context, axis=-1, keepdims=True) + epsilon)
    unit = context * inv
    unit_ref[...] = unit
    inv_ref[...] = jnp.broadcast_to(inv, inv_ref.shape)
    for p in range(shards):
        out_ref[p] = jnp.concatenate([sent_a_ref[p].astype(F32), unit], axis=0).astype(BF16)


def pair_body(place, scalars, got_ref, text_ref, d_image_ref, d_text_ref, loss_ref):
    loaders, got_rows, width = got_ref.shape
    slots = d_image_ref.shape[1]
    images = jnp.concatenate(
        [got_ref[s].astype(F32)[got_rows - slots :] for s in range(loaders)], axis=0
    ).astype(BF16)
    texts = text_ref[...]
    count = images.shape[0]
    text_count = texts.shape[0]
    scale = scalars[0]
    logits = scale * nt_dot(images, texts) + scalars[1]
    row = lax.broadcasted_iota(jnp.int32, (count, text_count), 0)
    column = lax.broadcasted_iota(jnp.int32, (count, text_count), 1)
    loader, owner = row // slots, row % slots
    matched = (owner == place[1]) & (column == place[0] * slots + loader)
    matched = matched.astype(F32)
    decay = jnp.exp(-jnp.abs(logits))
    signed = (1.0 - 2.0 * matched) * logits
    losses = jnp.maximum(signed, 0.0) + jnp.log1p(decay)
    sigmoid = jnp.where(logits >= 0.0, 1.0, decay) / (1.0 + decay)
    coefficient = (scale * (sigmoid - matched)).astype(BF16)
    d_image = jnp.dot(coefficient, texts, preferred_element_type=F32)
    d_image_ref[...] = d_image.reshape(d_image_ref.shape).astype(BF16)
    d_text = tn_dot(coefficient, images)
    d_text_ref[...] = d_text.reshape(d_text_ref.shape).astype(BF16)
    per_image = jnp.sum(losses, axis=-1, keepdims=True)
    per_owner = jnp.sum(per_image.reshape(loaders, slots, 1), axis=0)
    loss_ref[...] = jnp.broadcast_to(per_owner, loss_ref.shape)


def back_body(
    got_ref, unit_ref, invn_ref, full_ref, normed_ref, scaled_ref, inv_ref, w_ref, probe_ref,
    gain_ref, loss_ref, out_ref,
):
    slots, rows, width = normed_ref.shape
    heads = probe_ref.shape[0]
    cut = width // slots
    scale = 1.0 / math.sqrt(width // heads)
    d_image = jnp.sum(got_ref[...].astype(F32), axis=0)
    unit = unit_ref[...]
    along = jnp.sum(d_image * unit, axis=-1, keepdims=True)
    d_context = (d_image - unit * along) * invn_ref[:, 0:1]
    d_context = d_context.astype(BF16).astype(F32)
    spread = (d_context[:, None, :] * head_mask(heads, width)[None]).reshape(slots * heads, width)
    back = nt_dot(spread.astype(BF16), full_ref[...]).astype(BF16).reshape(slots, heads, width)
    gain = gain_ref[...]
    probe = probe_ref[...]
    probe_total = jnp.zeros((heads, width), F32)
    gain_total = jnp.zeros((8, width), F32)
    for r in range(slots):
        scaled = scaled_ref[r]
        weights = w_ref[r]
        d_weights = nt_dot(back[r], scaled)
        centre = jnp.sum(weights * d_weights, axis=-1, keepdims=True)
        d_scores = (weights * (d_weights - centre) * scale).astype(BF16)
        probe_total = probe_total + jnp.dot(d_scores, scaled, preferred_element_type=F32)
        d_scaled = tn_dot(
            jnp.concatenate([weights.astype(BF16), d_scores], axis=0),
            jnp.concatenate([back[r], probe], axis=0),
        )
        normed = normed_ref[r]
        gain_total = gain_total + jnp.sum((d_scaled * normed).reshape(rows // 8, 8, width), axis=0)
        grad_in = d_scaled * gain
        mean_a = jnp.sum(grad_in, axis=-1, keepdims=True) * (1.0 / width)
        mean_b = jnp.sum(grad_in * normed, axis=-1, keepdims=True) * (1.0 / width)
        row_grad = inv_ref[r][:, 0:1] * (grad_in - mean_a - normed * mean_b)
        out_ref[r, 0:rows, :] = row_grad.astype(BF16)
    gain_sum = jnp.sum(gain_total, axis=0, keepdims=True)
    loss = loss_ref[...]
    high = loss.astype(BF16).astype(F32)
    middle = (loss - high).astype(BF16).astype(F32)
    low = loss - high - middle
    for p in range(slots):
        lanes = slice(p * cut, (p + 1) * cut)
        pad = jnp.zeros((8, 256 - cut), F32)
        losses = jnp.concatenate(
            [high[p : p + 1], middle[p : p + 1], low[p : p + 1], jnp.zeros((5, 128), F32)], axis=0
        )
        misc = jnp.concatenate(
            [
                probe_total[0:8, lanes],
                pad,
                probe_total[8:16, lanes],
                pad,
                jnp.broadcast_to(gain_sum[:, lanes], (8, cut)),
                pad,
                losses,
                jnp.zeros((8, width - 896), F32),
            ],
            axis=1,
        )
        out_ref[p, rows : rows + 16, :] = jnp.concatenate([d_context, misc], axis=0).astype(BF16)


def last_body(got_ref, a_ref, row_ref, value_ref, probe_ref, gain_ref, loss_ref, *, texts):
    loaders, got_rows, width = got_ref.shape
    rows = row_ref.shape[2]
    heads, images, cut = a_ref.shape
    tails = []
    for s in range(loaders):
        row_ref[0, s] = got_ref[s, 0:rows, :]
        tails.append(got_ref[s, rows : rows + 16, :].astype(F32))
    d_context = jnp.concatenate([t[0:8] for t in tails], axis=0)
    mask = head_mask(heads, width)
    total = jnp.zeros((cut, width), F32)
    for h in range(heads):
        total = total + tn_dot(a_ref[h], (d_context * mask[h : h + 1]).astype(BF16))
    value_ref[0] = total.astype(BF16)
    misc = tails[0][8:16]
    for s in range(1, loaders):
        misc = misc + tails[s][8:16]
    probe_ref[...] = jnp.concatenate([misc[:, 0:cut], misc[:, 256 : 256 + cut]], axis=0).astype(BF16)
    gain_ref[...] = misc[0:1, 512 : 512 + cut].astype(BF16)
    loss_ref[...] = (misc[0:1, 768:769] + misc[1:2, 768:769] + misc[2:3, 768:769]) / texts


def local(
    patches, counts, owners, captions, norm_gain, key_probe, value_weight, logit_scale, logit_bias
):
    _, slots, rows, width = patches.shape
    heads = key_probe.shape[1]
    peers = lax.axis_size("fsdp")
    ranks = lax.axis_size("dp")
    cut = width // peers
    dp_index = lax.axis_index("dp")
    core = dp_index % 2
    place = jnp.stack([dp_index, lax.axis_index("fsdp"), core]).astype(jnp.int32)
    scalars = jnp.concatenate([logit_scale, logit_bias])
    gain = norm_gain.reshape(1, width)
    probe = key_probe.T

    start = core * (cut - SEND_ROWS)
    part = lax.dynamic_slice_in_dim(value_weight, start, SEND_ROWS, axis=0)
    mine = lax.all_to_all(
        jnp.broadcast_to(part[None], (peers, SEND_ROWS, width)), "fsdp", 0, 0, tiled=True
    )
    other = lax.ppermute(mine, "dp", [(i, i ^ 1) for i in range(ranks)])

    caption_f = captions[0].astype(F32)
    caption_inv = lax.rsqrt(jnp.sum(caption_f * caption_f, axis=-1, keepdims=True) + epsilon)
    caption_unit = caption_f * caption_inv
    texts = lax.all_gather(caption_unit.astype(BF16), "dp", axis=0, tiled=True)

    shape = jax.ShapeDtypeStruct
    normed, scaled, inv_std, weights, pooled = call(
        pool_body,
        [
            shape((slots, rows, width), F32),
            shape((slots, rows, width), BF16),
            shape((slots, rows, 128), F32),
            shape((slots, heads, rows), F32),
            shape((slots, heads, width), BF16),
        ],
        [sspec(), sspec(), vspec(), vspec(), vspec()],
        40_000_000,
        4_000_000,
        name="pool",
    )(owners[0], counts[0], patches[0], gain, probe)
    sent_pooled = (
        pooled.reshape(slots, heads, peers, cut)
        .transpose(2, 1, 0, 3)
        .reshape(peers, heads, slots * cut)
    )
    full, unit, inv_norm, sent = call(
        image_body,
        [
            shape((width, width), BF16),
            shape((slots, width), F32),
            shape((slots, 128), F32),
            shape((peers, heads + slots, width), BF16),
        ],
        [sspec(), vspec(), vspec(), vspec(), vspec()],
        400_000_000,
        6_000_000,
        name="image",
    )(place, mine, other, pooled, sent_pooled)
    got = lax.all_to_all(sent, "fsdp", 0, 0, tiled=True)
    d_image_part, d_text_part, loss_sums = call(
        pair_body,
        [
            shape((peers, slots, width), BF16),
            shape((ranks, slots, width), BF16),
            shape((slots, 128), F32),
        ],
        [sspec(), sspec(), vspec(), vspec()],
        120_000_000,
        2_000_000,
        name="pair",
    )(place, scalars, got, texts)
    d_image_got = lax.all_to_all(d_image_part, "fsdp", 0, 0, tiled=True)
    d_text_got = lax.all_to_all(d_text_part, "dp", 0, 0, tiled=True)

    outgoing = call(
        back_body,
        [shape((peers, rows + 16, width), BF16)],
        [vspec()] * 11,
        500_000_000,
        8_000_000,
        name="back",
    )(
        d_image_got, unit, inv_norm, full, normed, scaled, inv_std, weights, probe, gain, loss_sums
    )[0]
    arrived = lax.all_to_all(outgoing, "fsdp", 0, 0, tiled=True)

    pooled_got = (
        got[:, :heads]
        .reshape(peers, heads, slots, cut)
        .transpose(1, 0, 2, 3)
        .reshape(heads, peers * slots, cut)
    )
    batch = ranks * peers * slots

    def last(*refs):
        last_body(*refs, texts=batch)

    row_grad, value_grad, probe_t, gain_grad, loss_part = call(
        last,
        [
            shape((1, slots, rows, width), BF16),
            shape((1, cut, width), BF16),
            shape((heads, cut), BF16),
            shape((1, cut), BF16),
            shape((1, 1), F32),
        ],
        [vspec(), vspec()],
        400_000_000,
        3_000_000,
        name="last",
    )(arrived, pooled_got)

    d_caption = jnp.sum(d_text_got.astype(F32), axis=0)
    text_grad = (
        (d_caption - caption_unit * jnp.sum(d_caption * caption_unit, axis=-1, keepdims=True))
        * caption_inv
    ).astype(BF16)
    return (loss_part, row_grad, text_grad[None], value_grad, probe_t.T[None], gain_grad)


def solution(mesh):
    placed = (
        P(("dp", "fsdp"), None, None, None),
        P(("dp", "fsdp"), None),
        P(("dp", "fsdp"), None),
        P(("dp", "fsdp"), None, None),
        P(),
        P(),
        P("fsdp", None),
        P(),
        P(),
    )
    return jax.shard_map(
        local,
        mesh=mesh,
        in_specs=placed,
        out_specs=(
            P("dp", "fsdp"),
            P(("dp", "fsdp"), None, None, None),
            P(("dp", "fsdp"), None, None),
            P("dp", "fsdp", None),
            P("dp", "fsdp", None),
            P("dp", "fsdp"),
        ),
        check_vma=False,
    )
```

```python
import math

import jax
import jax.numpy as jnp
from jax import lax
from jax.experimental import pallas as pl
from jax.experimental.pallas import tpu as pltpu
from jax.sharding import PartitionSpec as P

epsilon = 1e-06
F32 = jnp.float32
BF16 = jnp.bfloat16

VMEM_LIMIT = 16 * 1024 * 1024
VMEM_LARGE = 60_180_000
SEND_ROWS = 80


TEXT_BITS = (8, 4, 2, 16, 1)


def swapped(block, bit):
    return lax.ppermute(block, "dp", [(i, i ^ bit) for i in range(lax.axis_size("dp"))])


def vspec():
    return pl.BlockSpec(memory_space=pltpu.VMEM)


def sspec():
    return pl.BlockSpec(memory_space=pltpu.SMEM)


def hspec():
    return pl.BlockSpec(memory_space=pltpu.HBM)


def call(body, outs, in_specs, flops, nbytes, scratch=(), name=None, limit=VMEM_LIMIT):
    return pl.pallas_call(
        body,
        out_shape=[shape for shape, _ in outs],
        in_specs=in_specs,
        out_specs=[spec for _, spec in outs],
        scratch_shapes=list(scratch),
        compiler_params=pltpu.CompilerParams(vmem_limit_bytes=limit),
        cost_estimate=pl.CostEstimate(flops=flops, bytes_accessed=nbytes, transcendentals=0),
        name=name,
    )


def source_of(owners, owner, slots):
    source = jnp.int32(0)
    for k in range(slots):
        source = source + jnp.where(owners[k] == owner, k, 0)
    return source


def nt_dot(a, b):
    return lax.dot_general(a, b, (((1,), (1,)), ((), ())), preferred_element_type=F32)


def tn_dot(a, b):
    return lax.dot_general(a, b, (((0,), (0,)), ((), ())), preferred_element_type=F32)


def head_mask(heads, width):
    head_width = width // heads
    low = lax.broadcasted_iota(jnp.int32, (heads, width), 0) * head_width
    column = lax.broadcasted_iota(jnp.int32, (heads, width), 1)
    return ((column >= low) & (column < low + head_width)).astype(F32)


def pool_body(owners, counts, x_ref, gain_ref, probe_ref, stats_ref, w_ref, a_ref, scaled_ref):
    slots, rows, width = x_ref.shape
    heads = probe_ref.shape[0]
    scale = 1.0 / math.sqrt(width // heads)
    gain = gain_ref[...]
    lanes = slots * heads
    column = lax.broadcasted_iota(jnp.int32, (rows, lanes), 1)
    patch = lax.broadcasted_iota(jnp.int32, (rows, lanes), 0)
    masks = []
    for r in range(slots):
        source = source_of(owners, r, slots)
        x = x_ref[source].astype(F32)
        mean = jnp.sum(x, axis=-1, keepdims=True) * (1.0 / width)
        centered = x - mean
        var = jnp.sum(centered * centered, axis=-1, keepdims=True) * (1.0 / width)
        inv = lax.rsqrt(var + epsilon)
        scaled_ref[r * rows : (r + 1) * rows, :] = ((centered * inv) * gain).astype(BF16)
        stats_ref[r * rows : (r + 1) * rows, :] = jnp.where(column < lanes // 2, mean, inv)
        own = (column >= r * heads) & (column < (r + 1) * heads)
        masks.append(jnp.where(own & (patch < counts[source]), 1.0, 0.0))
    valid = jnp.concatenate(masks, axis=0) > 0.5
    scaled = scaled_ref[...]
    tiled = jnp.concatenate([probe_ref[...].astype(F32)] * slots, axis=0).astype(BF16)
    scores = nt_dot(scaled, tiled) * scale
    highest = jnp.max(jnp.where(valid, scores, -jnp.inf), axis=0, keepdims=True)
    raised = jnp.where(valid, jnp.exp(jnp.where(valid, scores - highest, 0.0)), 0.0)
    weights = raised / jnp.sum(raised, axis=0, keepdims=True)
    w_ref[...] = weights
    a_ref[...] = tn_dot(weights.astype(BF16), scaled).astype(BF16)


def image_body(
    mine_ref, other_ref, a_ref, full_out, unit_ref, inv_ref, out_ref, full, sem
):
    shards, part_rows, width = mine_ref.shape
    slots = unit_ref.shape[0]
    heads = a_ref.shape[0] // slots
    cut = width // shards
    rest = cut - part_rows
    core = lax.rem(lax.axis_index("dp"), 2)

    def put(low_ref, high_ref):
        for j in range(shards):
            full[j * cut : j * cut + part_rows, :] = low_ref[j]
            full[j * cut + part_rows : (j + 1) * cut, :] = high_ref[j, part_rows - rest :, :]

    @pl.when(core == 0)
    def _():
        put(mine_ref, other_ref)

    @pl.when(core != 0)
    def _():
        put(other_ref, mine_ref)

    copy = pltpu.make_async_copy(full, full_out, sem)
    copy.start()
    pooled = a_ref[...]
    wide = jnp.dot(pooled, full[...], preferred_element_type=F32).reshape(slots, heads, width)
    context = jnp.sum(wide * head_mask(heads, width)[None], axis=1)
    inv = lax.rsqrt(jnp.sum(context * context, axis=-1, keepdims=True) + epsilon)
    unit = context * inv
    unit_ref[...] = unit
    inv_ref[...] = jnp.broadcast_to(inv, inv_ref.shape)
    wide_pooled = pooled.astype(F32)
    for p in range(shards):
        moved = jnp.concatenate(
            [
                wide_pooled[b * heads : (b + 1) * heads, p * cut : (p + 1) * cut]
                for b in range(slots)
            ],
            axis=1,
        )
        out_ref[p] = jnp.concatenate([moved, unit], axis=0).astype(BF16)
    copy.wait()


def pair_body(place, scalars, got_ref, text_ref, d_image_ref, keep_ref, send_ref, loss_ref):
    loaders, got_rows, width = got_ref.shape
    slots = d_image_ref.shape[1]
    images = jnp.concatenate(
        [got_ref[s].astype(F32)[got_rows - slots :] for s in range(loaders)], axis=0
    ).astype(BF16)
    texts = text_ref[...]
    count = images.shape[0]
    text_count = texts.shape[0]
    scale = scalars[0]
    logits = scale * nt_dot(images, texts) + scalars[1]
    row = lax.broadcasted_iota(jnp.int32, (count, text_count), 0)
    column = lax.broadcasted_iota(jnp.int32, (count, text_count), 1)
    loader, owner = row // slots, row % slots
    matched = (owner == place[0]) & (column == loader)
    matched = matched.astype(F32)
    decay = jnp.exp(-jnp.abs(logits))
    signed = (1.0 - 2.0 * matched) * logits
    losses = jnp.maximum(signed, 0.0) + jnp.log1p(decay)
    sigmoid = jnp.where(logits >= 0.0, 1.0, decay) / (1.0 + decay)
    coefficient = (scale * (sigmoid - matched)).astype(BF16)
    d_image = jnp.dot(coefficient, texts, preferred_element_type=F32)
    d_image_ref[...] = d_image.reshape(d_image_ref.shape).astype(BF16)
    d_text = tn_dot(coefficient, images)
    keep_ref[...] = d_text[: text_count // 2]
    send_ref[...] = d_text[text_count // 2 :].astype(BF16)
    per_image = jnp.sum(losses, axis=-1, keepdims=True)
    per_owner = jnp.sum(per_image.reshape(loaders, slots, 1), axis=0)
    loss_ref[...] = jnp.broadcast_to(per_owner, loss_ref.shape)


def back_body(
    owners, got_ref, unit_ref, invn_ref, full_in, x_in, stats_in, w_in, probe_ref, gain_ref, loss_ref,
    out_ref, full, x_ref, stats_ref, w_ref, normed_ref, scaled_ref, right, result, sems,
):
    slots, rows, width = x_ref.shape
    heads = probe_ref.shape[0]
    lanes = slots * heads
    cut = width // slots
    scale = 1.0 / math.sqrt(width // heads)
    chunk = width // 3
    patches = [
        pltpu.make_async_copy(x_in.at[0, source_of(owners, r, slots)], x_ref.at[r], sems.at[r])
        for r in range(slots)
    ]
    small = [
        pltpu.make_async_copy(stats_in, stats_ref, sems.at[slots]),
        pltpu.make_async_copy(w_in, w_ref, sems.at[slots + 1]),
    ]
    values = [
        pltpu.make_async_copy(
            full_in.at[pl.ds(c * chunk, chunk), :],
            full.at[pl.ds(c * chunk, chunk), :],
            sems.at[slots + 2 + c],
        )
        for c in range(3)
    ]
    for copy in small[:1] + patches + values + small[1:]:
        copy.start()
    d_image = jnp.sum(got_ref[...].astype(F32), axis=0)
    unit = unit_ref[...]
    along = jnp.sum(d_image * unit, axis=-1, keepdims=True)
    d_context = (d_image - unit * along) * invn_ref[:, 0:1]
    d_context = d_context.astype(BF16).astype(F32)
    spread = (d_context[:, None, :] * head_mask(heads, width)[None]).reshape(lanes, width).astype(BF16)
    gain = gain_ref[...]
    right[lanes:, :] = jnp.concatenate([probe_ref[...].astype(F32)] * slots, axis=0).astype(BF16)
    small[0].wait()
    for r in range(slots):
        patches[r].wait()
        at = slice(r * rows, (r + 1) * rows)
        normed = (x_ref[r].astype(F32) - stats_ref[at, 0:1]) * stats_ref[at, lanes // 2 : lanes // 2 + 1]
        normed_ref[at, :] = normed
        scaled_ref[at, :] = (normed * gain).astype(BF16)
    for c in range(3):
        values[c].wait()
        at = slice(c * chunk, (c + 1) * chunk)
        right[0:lanes, at] = nt_dot(spread, full[at, :]).astype(BF16)
    small[1].wait()
    scaled = scaled_ref[...]
    weights = w_ref[...]
    d_weights = nt_dot(scaled, right[0:lanes, :])
    centre = jnp.sum(weights * d_weights, axis=0, keepdims=True)
    d_scores = (weights * (d_weights - centre) * scale).astype(BF16)
    left = jnp.concatenate([weights.astype(BF16), d_scores], axis=1)
    gain_total = jnp.zeros((8, width), F32)
    sent = []
    half = slots // 2
    for g in range(2):
        d_scaled_half = jnp.dot(
            left[g * half * rows : (g + 1) * half * rows], right[...], preferred_element_type=F32
        )
        for k in range(half):
            r = g * half + k
            at = slice(r * rows, (r + 1) * rows)
            d_scaled = d_scaled_half[k * rows : (k + 1) * rows]
            normed = normed_ref[at, :]
            product = d_scaled * normed
            gain_total = gain_total + jnp.sum(product.reshape(rows // 8, 8, width), axis=0)
            grad_in = d_scaled * gain
            mean_a = jnp.sum(grad_in, axis=-1, keepdims=True) * (1.0 / width)
            mean_b = jnp.sum(product * gain, axis=-1, keepdims=True) * (1.0 / width)
            inv = stats_ref[at, lanes // 2 : lanes // 2 + 1]
            result[r, 0:rows, :] = (inv * (grad_in - mean_a - normed * mean_b)).astype(BF16)
        at = pl.ds(g * half, half)
        copy = pltpu.make_async_copy(
            result.at[at, pl.ds(0, rows), :], out_ref.at[at, pl.ds(0, rows), :], sems.at[slots + 5 + g]
        )
        copy.start()
        sent.append(copy)
    probe_total = jnp.sum(tn_dot(d_scores, scaled).reshape(slots, heads, width), axis=0)
    gain_sum = jnp.sum(gain_total, axis=0, keepdims=True)
    loss = loss_ref[...]
    high = loss.astype(BF16).astype(F32)
    middle = (loss - high).astype(BF16).astype(F32)
    low = loss - high - middle
    pad = jnp.zeros((8, 256 - cut), F32)
    for p in range(slots):
        at = slice(p * cut, (p + 1) * cut)
        losses = jnp.concatenate(
            [high[p : p + 1], middle[p : p + 1], low[p : p + 1], jnp.zeros((5, 128), F32)], axis=0
        )
        misc = jnp.concatenate(
            [
                probe_total[0:8, at],
                pad,
                probe_total[8:16, at],
                pad,
                jnp.broadcast_to(gain_sum[:, at], (8, cut)),
                pad,
                losses,
                jnp.zeros((8, width - 896), F32),
            ],
            axis=1,
        )
        result[p, rows : rows + 16, :] = jnp.concatenate([d_context, misc], axis=0).astype(BF16)
    tail = pl.ds(rows, 16)
    copy = pltpu.make_async_copy(
        result.at[:, tail, :], out_ref.at[:, tail, :], sems.at[slots + 7]
    )
    copy.start()
    for copy in sent + [copy]:
        copy.wait()


def last_body(got_ref, a_ref, row_ref, value_ref, probe_ref, gain_ref, loss_ref, tail, sems, *, texts):
    loaders, got_rows, width = got_ref.shape
    rows = row_ref.shape[2]
    heads, images, cut = a_ref.shape
    head_width = width // heads
    first = pltpu.make_async_copy(got_ref.at[:, pl.ds(rows, 16), :], tail, sems.at[0])
    first.start()
    second = pltpu.make_async_copy(got_ref.at[:, pl.ds(0, rows), :], row_ref.at[0], sems.at[1])
    second.start()
    first.wait()
    tails = [tail[s].astype(F32) for s in range(loaders)]
    d_context = jnp.concatenate([t[0:8] for t in tails], axis=0)
    mask = head_mask(heads, width)
    tiles = [None] * (width // 128)
    for h in range(heads):
        low, high = h * head_width // 128, -(-(h + 1) * head_width // 128)
        lanes = slice(low * 128, high * 128)
        part = tn_dot(a_ref[h], (d_context[:, lanes] * mask[h : h + 1, lanes]).astype(BF16))
        for t in range(low, high):
            piece = part[:, (t - low) * 128 : (t - low + 1) * 128]
            tiles[t] = piece if tiles[t] is None else tiles[t] + piece
    value_ref[0] = jnp.concatenate(tiles, axis=1).astype(BF16)
    misc = tails[0][8:16]
    for s in range(1, loaders):
        misc = misc + tails[s][8:16]
    probe_ref[...] = jnp.concatenate([misc[:, 0:cut], misc[:, 256 : 256 + cut]], axis=0).astype(BF16)
    gain_ref[...] = misc[0:1, 512 : 512 + cut].astype(BF16)
    loss_ref[...] = (misc[0:1, 768:769] + misc[1:2, 768:769] + misc[2:3, 768:769]) / texts
    second.wait()


def local(
    patches, counts, owners, captions, norm_gain, key_probe, value_weight, logit_scale, logit_bias
):
    _, slots, rows, width = patches.shape
    heads = key_probe.shape[1]
    peers = lax.axis_size("fsdp")
    ranks = lax.axis_size("dp")
    cut = width // peers
    core = lax.axis_index("dp") % 2
    place = lax.axis_index("fsdp").astype(jnp.int32).reshape(1)
    scalars = jnp.concatenate([logit_scale, logit_bias])
    gain = norm_gain.reshape(1, width)
    probe = key_probe.T
    shape = jax.ShapeDtypeStruct
    dma = pltpu.SemaphoreType.DMA

    start = core * (cut - SEND_ROWS)
    part = lax.dynamic_slice_in_dim(value_weight, start, SEND_ROWS, axis=0)
    mine = lax.all_to_all(
        jnp.broadcast_to(part[None], (peers, SEND_ROWS, width)), "fsdp", 0, 0, tiled=True
    )

    lanes = slots * heads
    stats, weights, pooled = call(
        pool_body,
        [
            (shape((slots * rows, lanes), F32), vspec()),
            (shape((slots * rows, lanes), F32), vspec()),
            (shape((lanes, width), BF16), vspec()),
        ],
        [sspec(), sspec(), vspec(), vspec(), vspec()],
        40_000_000,
        4_000_000,
        [pltpu.VMEM((slots * rows, width), BF16)],
        name="pool",
    )(owners[0], counts[0], patches[0], gain, probe)

    caption_f = captions[0].astype(F32)
    caption_inv = lax.rsqrt(jnp.sum(caption_f * caption_f, axis=-1, keepdims=True) + epsilon)
    caption_unit = caption_f * caption_inv
    texts, pooled = lax.optimization_barrier((caption_unit.astype(BF16), pooled))
    for bit in [bit for bit in TEXT_BITS[:4] if bit < ranks]:
        texts = jnp.concatenate([texts, swapped(texts, bit)], axis=0)
    mine, texts = lax.optimization_barrier((mine, texts))
    other = swapped(mine, 1)
    for bit in [bit for bit in TEXT_BITS[4:] if bit < ranks]:
        texts = jnp.concatenate([texts, swapped(texts, bit)], axis=0)
    full, unit, inv_norm, sent = call(
        image_body,
        [
            (shape((width, width), BF16), hspec()),
            (shape((slots, width), F32), vspec()),
            (shape((slots, 128), F32), vspec()),
            (shape((peers, heads + slots, width), BF16), vspec()),
        ],
        [vspec()] * 3,
        400_000_000,
        6_000_000,
        [pltpu.VMEM((width, width), BF16), dma(())],
        name="image",
        limit=VMEM_LARGE,
    )(mine, other, pooled)
    got = lax.all_to_all(sent, "fsdp", 0, 0, tiled=True)
    half = ranks * slots // 2
    d_image_part, keep, send, loss_sums = call(
        pair_body,
        [
            (shape((peers, slots, width), BF16), vspec()),
            (shape((half, width), F32), vspec()),
            (shape((half, width), BF16), vspec()),
            (shape((slots, 128), F32), vspec()),
        ],
        [sspec(), sspec(), vspec(), vspec()],
        120_000_000,
        2_000_000,
        name="pair",
    )(place, scalars, got, texts)
    d_image_got = lax.all_to_all(d_image_part, "fsdp", 0, 0, tiled=True)

    def fold(total, bit):
        if bit >= ranks:
            return total
        rest = total.shape[0] // 2
        return total[:rest] + swapped(total[rest:].astype(BF16), bit).astype(F32)

    d_text = keep + swapped(send, TEXT_BITS[4]).astype(F32)
    d_text = fold(d_text, TEXT_BITS[3])
    d_image_got, d_text = lax.optimization_barrier((d_image_got, d_text))
    d_text = fold(d_text, TEXT_BITS[2])

    outgoing = call(
        back_body,
        [(shape((peers, rows + 16, width), BF16), hspec())],
        [sspec()] + [vspec()] * 3 + [hspec()] * 4 + [vspec()] * 3,
        500_000_000,
        8_000_000,
        [
            pltpu.VMEM((width, width), BF16),
            pltpu.VMEM((slots, rows, width), BF16),
            pltpu.VMEM((slots * rows, lanes), F32),
            pltpu.VMEM((slots * rows, lanes), F32),
            pltpu.VMEM((slots * rows, width), F32),
            pltpu.VMEM((slots * rows, width), BF16),
            pltpu.VMEM((2 * lanes, width), BF16),
            pltpu.VMEM((peers, rows + 16, width), BF16),
            dma((slots + 8,)),
        ],
        name="back",
        limit=VMEM_LARGE,
    )(
        owners[0], d_image_got, unit, inv_norm, full, patches, stats, weights, probe, gain, loss_sums
    )[0]
    outgoing, d_text = lax.optimization_barrier((outgoing, d_text))
    arrived = lax.all_to_all(outgoing, "fsdp", 0, 0, tiled=True)
    d_caption = fold(fold(d_text, TEXT_BITS[1]), TEXT_BITS[0])

    pooled_got = (
        got[:, :heads]
        .reshape(peers, heads, slots, cut)
        .transpose(1, 0, 2, 3)
        .reshape(heads, peers * slots, cut)
    )
    batch = ranks * peers * slots

    def last(*refs):
        last_body(*refs, texts=batch)

    row_grad, value_grad, probe_t, gain_grad, loss_part = call(
        last,
        [
            (shape((1, slots, rows, width), BF16), hspec()),
            (shape((1, cut, width), BF16), vspec()),
            (shape((heads, cut), BF16), vspec()),
            (shape((1, cut), BF16), vspec()),
            (shape((1, 1), F32), vspec()),
        ],
        [hspec(), vspec()],
        400_000_000,
        3_000_000,
        [pltpu.VMEM((peers, 16, width), BF16), dma((2,))],
        name="last",
    )(arrived, pooled_got)

    text_grad = (
        (d_caption - caption_unit * jnp.sum(d_caption * caption_unit, axis=-1, keepdims=True))
        * caption_inv
    ).astype(BF16)
    return (loss_part, row_grad, text_grad[None], value_grad, probe_t.T[None], gain_grad)


def solution(mesh):
    placed = (
        P(("dp", "fsdp"), None, None, None),
        P(("dp", "fsdp"), None),
        P(("dp", "fsdp"), None),
        P(("dp", "fsdp"), None, None),
        P(),
        P(),
        P("fsdp", None),
        P(),
        P(),
    )
    return jax.shard_map(
        local,
        mesh=mesh,
        in_specs=placed,
        out_specs=(
            P("dp", "fsdp"),
            P(("dp", "fsdp"), None, None, None),
            P(("dp", "fsdp"), None, None),
            P("dp", "fsdp", None),
            P("dp", "fsdp", None),
            P("dp", "fsdp"),
        ),
        check_vma=False,
    )
```

```python
import math

import jax
import jax.numpy as jnp
from jax import lax
from jax.experimental import pallas as pl
from jax.experimental.pallas import tpu as pltpu
from jax.sharding import PartitionSpec as P

epsilon = 1e-06
F32 = jnp.float32
BF16 = jnp.bfloat16

VMEM_LIMIT = 16 * 1024 * 1024
VMEM_LARGE = 60_000_000
VMEM_IMAGE = 28_000_000
STASH_ROWS = 15_616
SEND_ROWS = 72


Z_BITS = (8, 4, 12)
NEXT_BIT, SIDE_BIT, CORE_BIT = 2, 16, 1


def swapped(block, bit):
    return lax.ppermute(block, "dp", [(i, i ^ bit) for i in range(lax.axis_size("dp"))])


def vspec():
    return pl.BlockSpec(memory_space=pltpu.VMEM)


def sspec():
    return pl.BlockSpec(memory_space=pltpu.SMEM)


def hspec():
    return pl.BlockSpec(memory_space=pltpu.HBM)


def call(body, outs, in_specs, flops, nbytes, scratch=(), name=None, limit=VMEM_LIMIT):
    return pl.pallas_call(
        body,
        out_shape=[shape for shape, _ in outs],
        in_specs=in_specs,
        out_specs=[spec for _, spec in outs],
        scratch_shapes=list(scratch),
        compiler_params=pltpu.CompilerParams(vmem_limit_bytes=limit),
        cost_estimate=pl.CostEstimate(flops=flops, bytes_accessed=nbytes, transcendentals=0),
        name=name,
    )


def source_of(owners, owner, slots):
    source = jnp.int32(0)
    for k in range(slots):
        source = source + jnp.where(owners[k] == owner, k, 0)
    return source


def nt_dot(a, b):
    return lax.dot_general(a, b, (((1,), (1,)), ((), ())), preferred_element_type=F32)


def tn_dot(a, b):
    return lax.dot_general(a, b, (((0,), (0,)), ((), ())), preferred_element_type=F32)


def head_mask(heads, width):
    head_width = width // heads
    low = lax.broadcasted_iota(jnp.int32, (heads, width), 0) * head_width
    column = lax.broadcasted_iota(jnp.int32, (heads, width), 1)
    return ((column >= low) & (column < low + head_width)).astype(F32)


def pool_body(owners, counts, x_ref, gain_ref, probe_ref, stats_ref, w_ref, a_ref, scaled_ref):
    slots, rows, width = x_ref.shape
    heads = probe_ref.shape[0]
    scale = 1.0 / math.sqrt(width // heads)
    gain = gain_ref[...]
    lanes = slots * heads
    column = lax.broadcasted_iota(jnp.int32, (rows, lanes), 1)
    patch = lax.broadcasted_iota(jnp.int32, (rows, lanes), 0)
    masks = []
    for r in range(slots):
        source = source_of(owners, r, slots)
        x = x_ref[source].astype(F32)
        mean = jnp.sum(x, axis=-1, keepdims=True) * (1.0 / width)
        centered = x - mean
        var = jnp.sum(centered * centered, axis=-1, keepdims=True) * (1.0 / width)
        inv = lax.rsqrt(var + epsilon)
        scaled_ref[r * rows : (r + 1) * rows, :] = ((centered * inv) * gain).astype(BF16)
        stats_ref[r * rows : (r + 1) * rows, :] = jnp.where(column < lanes // 2, mean, inv)
        own = (column >= r * heads) & (column < (r + 1) * heads)
        masks.append(jnp.where(own & (patch < counts[source]), 1.0, 0.0))
    valid = jnp.concatenate(masks, axis=0) > 0.5
    scaled = scaled_ref[...]
    tiled = jnp.concatenate([probe_ref[...].astype(F32)] * slots, axis=0).astype(BF16)
    scores = nt_dot(scaled, tiled) * scale
    highest = jnp.max(jnp.where(valid, scores, -jnp.inf), axis=0, keepdims=True)
    raised = jnp.where(valid, jnp.exp(jnp.where(valid, scores - highest, 0.0)), 0.0)
    weights = raised / jnp.sum(raised, axis=0, keepdims=True)
    w_ref[...] = weights
    a_ref[...] = tn_dot(weights.astype(BF16), scaled).astype(BF16)


def image_body(
    mine_ref, other_ref, a_ref, full_out, unit_ref, inv_ref, out_ref, full, sem
):
    shards, part_rows, width = mine_ref.shape
    slots = unit_ref.shape[0]
    heads = a_ref.shape[0] // slots
    cut = width // shards
    rest = cut - part_rows
    core = lax.rem(lax.axis_index("dp"), 2)

    def put(low_ref, high_ref):
        for j in range(shards):
            full[j * cut : j * cut + part_rows, :] = low_ref[j]
            full[j * cut + part_rows : (j + 1) * cut, :] = high_ref[j, part_rows - rest :, :]

    @pl.when(core == 0)
    def _():
        put(mine_ref, other_ref)

    @pl.when(core != 0)
    def _():
        put(other_ref, mine_ref)

    copy = pltpu.make_async_copy(full, full_out.at[pl.ds(0, width), :], sem)
    copy.start()
    pooled = a_ref[...]
    wide = jnp.dot(pooled, full[...], preferred_element_type=F32).reshape(slots, heads, width)
    context = jnp.sum(wide * head_mask(heads, width)[None], axis=1)
    inv = lax.rsqrt(jnp.sum(context * context, axis=-1, keepdims=True) + epsilon)
    unit = context * inv
    unit_ref[...] = unit
    inv_ref[...] = jnp.broadcast_to(inv, inv_ref.shape)
    wide_pooled = pooled.astype(F32)
    for p in range(shards):
        moved = jnp.concatenate(
            [
                wide_pooled[b * heads : (b + 1) * heads, p * cut : (p + 1) * cut]
                for b in range(slots)
            ],
            axis=1,
        )
        out_ref[p] = jnp.concatenate([moved, unit], axis=0).astype(BF16)
    copy.wait()


def caption_body(caption_ref, unit_ref, inv_ref, text_ref):
    caption = caption_ref[...].astype(F32)
    inv = lax.rsqrt(jnp.sum(caption * caption, axis=-1, keepdims=True) + epsilon)
    unit = caption * inv
    unit_ref[...] = unit
    inv_ref[...] = jnp.broadcast_to(inv, inv_ref.shape)
    text_ref[...] = unit.astype(BF16)


def pair_body(place, scalars, got_ref, text_ref, d_image_ref, coefficient_ref, image_ref, loss_ref):
    loaders, got_rows, width = got_ref.shape
    slots = d_image_ref.shape[1]
    images = jnp.concatenate(
        [got_ref[s].astype(F32)[got_rows - slots :] for s in range(loaders)], axis=0
    ).astype(BF16)
    image_ref[...] = images
    texts = text_ref[...]
    count = images.shape[0]
    text_count = texts.shape[0]
    scale = scalars[0]
    logits = scale * nt_dot(images, texts) + scalars[1]
    row = lax.broadcasted_iota(jnp.int32, (count, text_count), 0)
    column = lax.broadcasted_iota(jnp.int32, (count, text_count), 1)
    loader, owner = row // slots, row % slots
    matched = (owner == place[0]) & (column == loader)
    matched = matched.astype(F32)
    decay = jnp.exp(-jnp.abs(logits))
    signed = (1.0 - 2.0 * matched) * logits
    losses = jnp.maximum(signed, 0.0) + jnp.log1p(decay)
    sigmoid = jnp.where(logits >= 0.0, 1.0, decay) / (1.0 + decay)
    coefficient = (scale * (sigmoid - matched)).astype(BF16)
    coefficient_ref[...] = coefficient
    d_image = jnp.dot(coefficient, texts, preferred_element_type=F32)
    d_image_ref[...] = d_image.reshape(d_image_ref.shape).astype(BF16)
    per_image = jnp.sum(losses, axis=-1, keepdims=True)
    per_owner = jnp.sum(per_image.reshape(loaders, slots, 1), axis=0)
    loss_ref[...] = jnp.broadcast_to(per_owner, loss_ref.shape)


def text_body(coefficient_ref, image_ref, keep_ref, send_ref):
    d_text = tn_dot(coefficient_ref[...], image_ref[...])
    half = keep_ref.shape[0]
    keep_ref[...] = d_text[:half]
    send_ref[...] = d_text[half:].astype(BF16)


def fold_body(total_ref, got_ref, keep_ref, send_ref):
    total = total_ref[...] + got_ref[...].astype(F32)
    half = keep_ref.shape[0]
    keep_ref[...] = total[:half]
    send_ref[...] = total[half:].astype(BF16)


def split_body(total_ref, got_ref, keep_ref, *block_refs):
    total = total_ref[...] + got_ref[...].astype(F32)
    rows = keep_ref.shape[0]
    keep_ref[...] = total[:rows]
    for k, block_ref in enumerate(block_refs):
        block_ref[...] = total[(k + 1) * rows : (k + 2) * rows].astype(BF16)


def back_body(
    owners, got_in, unit_in, invn_in, full_in, x_in, stats_in, w_in, probe_in, gain_in, loss_in,
    out_ref, got_ref, unit_ref, invn_ref, probe_ref, gain_ref, loss_ref,
    full, x_ref, stats_ref, w_ref, normed_ref, scaled_ref, right, result, sems, extra_sems,
):
    slots, rows, width = x_ref.shape
    heads = probe_ref.shape[0]
    lanes = slots * heads
    cut = width // slots
    scale = 1.0 / math.sqrt(width // heads)
    chunk = width // 3
    patches = [
        pltpu.make_async_copy(x_in.at[0, source_of(owners, r, slots)], x_ref.at[r], sems.at[r])
        for r in range(slots)
    ]
    small = [
        pltpu.make_async_copy(stats_in, stats_ref, sems.at[slots]),
        pltpu.make_async_copy(w_in, w_ref, sems.at[slots + 1]),
    ]
    values = [
        pltpu.make_async_copy(
            full_in.at[pl.ds(c * chunk, chunk), :],
            full.at[pl.ds(c * chunk, chunk), :],
            sems.at[slots + 2 + c],
        )
        for c in range(3)
    ]
    pairs = [
        (got_in, got_ref),
        (unit_in, unit_ref),
        (invn_in, invn_ref),
        (probe_in, probe_ref),
        (gain_in, gain_ref),
        (loss_in, loss_ref),
    ]
    extra = [
        pltpu.make_async_copy(source, target, extra_sems.at[k])
        for k, (source, target) in enumerate(pairs)
    ]
    for copy in extra[:3] + small[:1] + extra[3:5] + patches + values + small[1:] + extra[5:]:
        copy.start()
    for copy in extra[:3]:
        copy.wait()
    d_image = jnp.sum(got_ref[...].astype(F32), axis=0)
    unit = unit_ref[...]
    along = jnp.sum(d_image * unit, axis=-1, keepdims=True)
    d_context = (d_image - unit * along) * invn_ref[:, 0:1]
    d_context = d_context.astype(BF16).astype(F32)
    spread = (d_context[:, None, :] * head_mask(heads, width)[None]).reshape(lanes, width).astype(BF16)
    for copy in extra[3:5]:
        copy.wait()
    gain = gain_ref[...]
    right[lanes:, :] = jnp.concatenate([probe_ref[...].astype(F32)] * slots, axis=0).astype(BF16)
    small[0].wait()
    for r in range(slots):
        patches[r].wait()
        at = slice(r * rows, (r + 1) * rows)
        normed = (x_ref[r].astype(F32) - stats_ref[at, 0:1]) * stats_ref[at, lanes // 2 : lanes // 2 + 1]
        normed_ref[at, :] = normed
        scaled_ref[at, :] = (normed * gain).astype(BF16)
    for c in range(3):
        values[c].wait()
        at = slice(c * chunk, (c + 1) * chunk)
        right[0:lanes, at] = nt_dot(spread, full[at, :]).astype(BF16)
    small[1].wait()
    scaled = scaled_ref[...]
    weights = w_ref[...]
    d_weights = nt_dot(scaled, right[0:lanes, :])
    centre = jnp.sum(weights * d_weights, axis=0, keepdims=True)
    d_scores = (weights * (d_weights - centre) * scale).astype(BF16)
    left = jnp.concatenate([weights.astype(BF16), d_scores], axis=1)
    gain_total = jnp.zeros((8, width), F32)
    sent = []
    half = slots // 2
    for g in range(2):
        d_scaled_half = jnp.dot(
            left[g * half * rows : (g + 1) * half * rows], right[...], preferred_element_type=F32
        )
        for k in range(half):
            r = g * half + k
            at = slice(r * rows, (r + 1) * rows)
            d_scaled = d_scaled_half[k * rows : (k + 1) * rows]
            normed = normed_ref[at, :]
            product = d_scaled * normed
            gain_total = gain_total + jnp.sum(product.reshape(rows // 8, 8, width), axis=0)
            grad_in = d_scaled * gain
            mean_a = jnp.sum(grad_in, axis=-1, keepdims=True) * (1.0 / width)
            mean_b = jnp.sum(product * gain, axis=-1, keepdims=True) * (1.0 / width)
            inv = stats_ref[at, lanes // 2 : lanes // 2 + 1]
            result[r, 0:rows, :] = (inv * (grad_in - mean_a - normed * mean_b)).astype(BF16)
        at = pl.ds(g * half, half)
        copy = pltpu.make_async_copy(
            result.at[at, pl.ds(0, rows), :], out_ref.at[at, pl.ds(0, rows), :], sems.at[slots + 5 + g]
        )
        copy.start()
        sent.append(copy)
    probe_total = jnp.sum(tn_dot(d_scores, scaled).reshape(slots, heads, width), axis=0)
    gain_sum = jnp.sum(gain_total, axis=0, keepdims=True)
    extra[5].wait()
    loss = loss_ref[...]
    high = loss.astype(BF16).astype(F32)
    middle = (loss - high).astype(BF16).astype(F32)
    low = loss - high - middle
    pad = jnp.zeros((8, 256 - cut), F32)
    for p in range(slots):
        at = slice(p * cut, (p + 1) * cut)
        losses = jnp.concatenate(
            [high[p : p + 1], middle[p : p + 1], low[p : p + 1], jnp.zeros((5, 128), F32)], axis=0
        )
        misc = jnp.concatenate(
            [
                probe_total[0:8, at],
                pad,
                probe_total[8:16, at],
                pad,
                jnp.broadcast_to(gain_sum[:, at], (8, cut)),
                pad,
                losses,
                jnp.zeros((8, width - 896), F32),
            ],
            axis=1,
        )
        result[p, rows : rows + 16, :] = jnp.concatenate([d_context, misc], axis=0).astype(BF16)
    tail = pl.ds(rows, 16)
    copy = pltpu.make_async_copy(
        result.at[:, tail, :], out_ref.at[:, tail, :], sems.at[slots + 7]
    )
    copy.start()
    for copy in sent + [copy]:
        copy.wait()


def last_body(got_ref, a_ref, row_ref, value_ref, probe_ref, gain_ref, loss_ref, tail, sems, *, texts):
    loaders, got_rows, width = got_ref.shape
    rows = row_ref.shape[2]
    heads, images, cut = a_ref.shape
    head_width = width // heads
    first = pltpu.make_async_copy(got_ref.at[:, pl.ds(rows, 16), :], tail, sems.at[0])
    first.start()
    second = pltpu.make_async_copy(got_ref.at[:, pl.ds(0, rows), :], row_ref.at[0], sems.at[1])
    second.start()
    first.wait()
    tails = [tail[s].astype(F32) for s in range(loaders)]
    d_context = jnp.concatenate([t[0:8] for t in tails], axis=0)
    mask = head_mask(heads, width)
    tiles = [None] * (width // 128)
    for h in range(heads):
        low, high = h * head_width // 128, -(-(h + 1) * head_width // 128)
        lanes = slice(low * 128, high * 128)
        part = tn_dot(a_ref[h], (d_context[:, lanes] * mask[h : h + 1, lanes]).astype(BF16))
        for t in range(low, high):
            piece = part[:, (t - low) * 128 : (t - low + 1) * 128]
            tiles[t] = piece if tiles[t] is None else tiles[t] + piece
    value_ref[0] = jnp.concatenate(tiles, axis=1).astype(BF16)
    misc = tails[0][8:16]
    for s in range(1, loaders):
        misc = misc + tails[s][8:16]
    probe_ref[...] = jnp.concatenate([misc[:, 0:cut], misc[:, 256 : 256 + cut]], axis=0).astype(BF16)
    gain_ref[...] = misc[0:1, 512 : 512 + cut].astype(BF16)
    loss_ref[...] = (misc[0:1, 768:769] + misc[1:2, 768:769] + misc[2:3, 768:769]) / texts
    second.wait()


def local(
    patches, counts, owners, captions, norm_gain, key_probe, value_weight, logit_scale, logit_bias
):
    _, slots, rows, width = patches.shape
    heads = key_probe.shape[1]
    peers = lax.axis_size("fsdp")
    ranks = lax.axis_size("dp")
    cut = width // peers
    core = lax.axis_index("dp") % 2
    place = lax.axis_index("fsdp").astype(jnp.int32).reshape(1)
    scalars = jnp.concatenate([logit_scale, logit_bias])
    gain = norm_gain.reshape(1, width)
    probe = key_probe.T
    shape = jax.ShapeDtypeStruct
    dma = pltpu.SemaphoreType.DMA

    start = core * (cut - SEND_ROWS)
    part = lax.dynamic_slice_in_dim(value_weight, start, SEND_ROWS, axis=0)
    mine = lax.all_to_all(
        jnp.broadcast_to(part[None], (peers, SEND_ROWS, width)), "fsdp", 0, 0, tiled=True
    )

    lanes = slots * heads
    stats, weights, pooled = call(
        pool_body,
        [
            (shape((slots * rows, lanes), F32), vspec()),
            (shape((slots * rows, lanes), F32), vspec()),
            (shape((lanes, width), BF16), vspec()),
        ],
        [sspec(), sspec(), vspec(), vspec(), vspec()],
        40_000_000,
        4_000_000,
        [pltpu.VMEM((slots * rows, width), BF16)],
        name="pool",
    )(owners[0], counts[0], patches[0], gain, probe)

    caption_unit, caption_inv, texts = call(
        caption_body,
        [
            (shape((slots, width), F32), vspec()),
            (shape((slots, 128), F32), vspec()),
            (shape((slots, width), BF16), vspec()),
        ],
        [vspec()],
        40_000_000,
        4_000_000,
        name="caption",
    )(captions[0])
    if ranks > 2:
        for bit in (8, 4, 2):
            texts = jnp.concatenate([texts, swapped(texts, bit)], axis=0)
    mine, texts, pooled = lax.optimization_barrier((mine, texts, pooled))
    other = swapped(mine, 1)
    if ranks > 2:
        side = swapped(texts, SIDE_BIT)
    full, unit, inv_norm, sent = call(
        image_body,
        [
            (shape((STASH_ROWS, width), BF16), hspec()),
            (shape((slots, width), F32), vspec()),
            (shape((slots, 128), F32), vspec()),
            (shape((peers, heads + slots, width), BF16), vspec()),
        ],
        [vspec()] * 3,
        400_000_000,
        6_000_000,
        [pltpu.VMEM((width, width), BF16), dma(())],
        name="image",
        limit=VMEM_IMAGE,
    )(mine, other, pooled)
    if ranks > 2:
        unit, side = lax.optimization_barrier((unit, side))
        texts = jnp.concatenate([texts, side], axis=0)
    got = lax.all_to_all(sent, "fsdp", 0, 0, tiled=True)
    texts = jnp.concatenate([texts, swapped(texts, CORE_BIT)], axis=0)
    count = peers * slots
    text_count = ranks * slots
    d_image_part, coefficient, images, loss_sums = call(
        pair_body,
        [
            (shape((peers, slots, width), BF16), vspec()),
            (shape((count, text_count), BF16), vspec()),
            (shape((count, width), BF16), vspec()),
            (shape((slots, 128), F32), vspec()),
        ],
        [sspec(), sspec(), vspec(), vspec()],
        80_000_000,
        2_000_000,
        name="pair",
    )(place, scalars, got, texts)
    d_image_got = lax.all_to_all(d_image_part, "fsdp", 0, 0, tiled=True)

    def halves(rows_out):
        return [
            (shape((rows_out, width), F32), vspec()),
            (shape((rows_out, width), BF16), vspec()),
        ]

    def fold(keep, send, bit):
        if bit >= ranks:
            return keep, send
        return call(
            fold_body, halves(keep.shape[0] // 2), [vspec(), vspec()], 40_000_000, 1_000_000, name="fold"
        )(keep, swapped(send, bit))

    keep, send = call(
        text_body, halves(text_count // 2), [vspec(), vspec()], 0, 0, name="text"
    )(coefficient, images)
    if ranks > 2:
        keep, send = fold(keep, send, CORE_BIT)
    d_image_got, keep, send = lax.optimization_barrier((d_image_got, keep, send))
    if ranks > 2:
        keep, send = fold(keep, send, SIDE_BIT)

    outgoing = call(
        back_body,
        [(shape((peers, rows + 16, width), BF16), hspec())],
        [sspec()] + [hspec()] * 10,
        500_000_000,
        8_000_000,
        [
            pltpu.VMEM((peers, slots, width), BF16),
            pltpu.VMEM((slots, width), F32),
            pltpu.VMEM((slots, 128), F32),
            pltpu.VMEM((heads, width), BF16),
            pltpu.VMEM((1, width), F32),
            pltpu.VMEM((slots, 128), F32),
            pltpu.VMEM((width, width), BF16),
            pltpu.VMEM((slots, rows, width), BF16),
            pltpu.VMEM((slots * rows, lanes), F32),
            pltpu.VMEM((slots * rows, lanes), F32),
            pltpu.VMEM((slots * rows, width), F32),
            pltpu.VMEM((slots * rows, width), BF16),
            pltpu.VMEM((2 * lanes, width), BF16),
            pltpu.VMEM((peers, rows + 16, width), BF16),
            dma((slots + 8,)),
            dma((6,)),
        ],
        name="back",
        limit=VMEM_LARGE,
    )(
        owners[0], d_image_got, unit, inv_norm, full, patches, stats, weights, probe, gain, loss_sums
    )[0]
    outgoing, keep, send = lax.optimization_barrier((outgoing, keep, send))
    arrived = lax.all_to_all(outgoing, "fsdp", 0, 0, tiled=True)
    if ranks > 2:
        d_caption, *blocks = call(
            split_body,
            [(shape((slots, width), F32), vspec())] + [(shape((slots, width), BF16), vspec())] * 3,
            [vspec(), vspec()],
            40_000_000,
            1_000_000,
            name="split",
        )(keep, swapped(send, NEXT_BIT))
        for block, bit in zip(blocks, Z_BITS):
            d_caption = d_caption + swapped(block, bit).astype(F32)
    else:
        d_caption = keep + swapped(send, CORE_BIT).astype(F32)

    pooled_got = (
        got[:, :heads]
        .reshape(peers, heads, slots, cut)
        .transpose(1, 0, 2, 3)
        .reshape(heads, peers * slots, cut)
    )
    batch = ranks * peers * slots

    def last(*refs):
        last_body(*refs, texts=batch)

    row_grad, value_grad, probe_t, gain_grad, loss_part = call(
        last,
        [
            (shape((1, slots, rows, width), BF16), hspec()),
            (shape((1, cut, width), BF16), vspec()),
            (shape((heads, cut), BF16), vspec()),
            (shape((1, cut), BF16), vspec()),
            (shape((1, 1), F32), vspec()),
        ],
        [hspec(), vspec()],
        400_000_000,
        3_000_000,
        [pltpu.VMEM((peers, 16, width), BF16), dma((2,))],
        name="last",
    )(arrived, pooled_got)

    text_grad = (
        (d_caption - caption_unit * jnp.sum(d_caption * caption_unit, axis=-1, keepdims=True))
        * caption_inv[:, 0:1]
    ).astype(BF16)
    return (loss_part, row_grad, text_grad[None], value_grad, probe_t.T[None], gain_grad)


def solution(mesh):
    placed = (
        P(("dp", "fsdp"), None, None, None),
        P(("dp", "fsdp"), None),
        P(("dp", "fsdp"), None),
        P(("dp", "fsdp"), None, None),
        P(),
        P(),
        P("fsdp", None),
        P(),
        P(),
    )
    return jax.shard_map(
        local,
        mesh=mesh,
        in_specs=placed,
        out_specs=(
            P("dp", "fsdp"),
            P(("dp", "fsdp"), None, None, None),
            P(("dp", "fsdp"), None, None),
            P("dp", "fsdp", None),
            P("dp", "fsdp", None),
            P("dp", "fsdp"),
        ),
        check_vma=False,
    )
```

```python
import math

import jax
import jax.numpy as jnp
from jax import lax
from jax.experimental import pallas as pl
from jax.experimental.pallas import tpu as pltpu
from jax.sharding import PartitionSpec as P

epsilon = 1e-06
F32 = jnp.float32
BF16 = jnp.bfloat16

VMEM_LIMIT = 16 * 1024 * 1024
VMEM_LARGE = 60_000_000
VMEM_IMAGE = 28_000_000
UNIT_ROWS = 48
STASH_ROWS = 15_616
SEND_ROWS = 72


Z_BITS = (8, 4, 12)
NEXT_BIT, SIDE_BIT, CORE_BIT = 2, 16, 1


def swapped(block, bit):
    return lax.ppermute(block, "dp", [(i, i ^ bit) for i in range(lax.axis_size("dp"))])


def vspec():
    return pl.BlockSpec(memory_space=pltpu.VMEM)


def sspec():
    return pl.BlockSpec(memory_space=pltpu.SMEM)


def hspec():
    return pl.BlockSpec(memory_space=pltpu.HBM)


def call(body, outs, in_specs, flops, nbytes, scratch=(), name=None, limit=VMEM_LIMIT):
    return pl.pallas_call(
        body,
        out_shape=[shape for shape, _ in outs],
        in_specs=in_specs,
        out_specs=[spec for _, spec in outs],
        scratch_shapes=list(scratch),
        compiler_params=pltpu.CompilerParams(vmem_limit_bytes=limit),
        cost_estimate=pl.CostEstimate(flops=flops, bytes_accessed=nbytes, transcendentals=0),
        name=name,
    )


def source_of(owners, owner, slots):
    source = jnp.int32(0)
    for k in range(slots):
        source = source + jnp.where(owners[k] == owner, k, 0)
    return source


def nt_dot(a, b):
    return lax.dot_general(a, b, (((1,), (1,)), ((), ())), preferred_element_type=F32)


def tn_dot(a, b):
    return lax.dot_general(a, b, (((0,), (0,)), ((), ())), preferred_element_type=F32)


def terms(value):
    high = value.astype(BF16).astype(F32)
    middle = (value - high).astype(BF16).astype(F32)
    return [high, middle, value - high - middle]


def head_mask(heads, width):
    head_width = width // heads
    low = lax.broadcasted_iota(jnp.int32, (heads, width), 0) * head_width
    column = lax.broadcasted_iota(jnp.int32, (heads, width), 1)
    return ((column >= low) & (column < low + head_width)).astype(F32)


def pool_body(owners, counts, x_ref, gain_ref, probe_ref, side_ref, a_ref, scaled_ref):
    slots, rows, width = x_ref.shape
    heads = probe_ref.shape[0]
    scale = 1.0 / math.sqrt(width // heads)
    gain = gain_ref[...]
    lanes = slots * heads
    column = lax.broadcasted_iota(jnp.int32, (rows, lanes), 1)
    patch = lax.broadcasted_iota(jnp.int32, (rows, lanes), 0)
    masks = []
    for r in range(slots):
        source = source_of(owners, r, slots)
        x = x_ref[source].astype(F32)
        mean = jnp.sum(x, axis=-1, keepdims=True) * (1.0 / width)
        centered = x - mean
        var = jnp.sum(centered * centered, axis=-1, keepdims=True) * (1.0 / width)
        inv = lax.rsqrt(var + epsilon)
        scaled_ref[r * rows : (r + 1) * rows, :] = ((centered * inv) * gain).astype(BF16)
        side_ref[r * rows : (r + 1) * rows, 0:lanes] = jnp.where(column < lanes // 2, mean, inv)
        own = (column >= r * heads) & (column < (r + 1) * heads)
        masks.append(jnp.where(own & (patch < counts[source]), 1.0, 0.0))
    valid = jnp.concatenate(masks, axis=0) > 0.5
    scaled = scaled_ref[...]
    tiled = jnp.concatenate([probe_ref[...].astype(F32)] * slots, axis=0).astype(BF16)
    scores = nt_dot(scaled, tiled) * scale
    highest = jnp.max(jnp.where(valid, scores, -jnp.inf), axis=0, keepdims=True)
    raised = jnp.where(valid, jnp.exp(jnp.where(valid, scores - highest, 0.0)), 0.0)
    weights = raised / jnp.sum(raised, axis=0, keepdims=True)
    side_ref[:, lanes:] = weights
    a_ref[...] = tn_dot(weights.astype(BF16), scaled).astype(BF16)


def image_body(
    mine_ref, other_ref, a_ref, full_out, out_ref, full, sems
):
    shards, part_rows, width = mine_ref.shape
    slots = shards
    heads = a_ref.shape[0] // slots
    cut = width // shards
    rest = cut - part_rows
    core = lax.rem(lax.axis_index("dp"), 2)

    def put(low_ref, high_ref):
        for j in range(shards):
            full[j * cut : j * cut + part_rows, :] = low_ref[j]
            full[j * cut + part_rows : (j + 1) * cut, :] = high_ref[j, part_rows - rest :, :]

    @pl.when(core == 0)
    def _():
        put(mine_ref, other_ref)

    @pl.when(core != 0)
    def _():
        put(other_ref, mine_ref)

    copies = [
        pltpu.make_async_copy(full.at[at, :], full_out.at[at, :], sems.at[k])
        for k, at in enumerate([pl.ds(0, width), pl.ds(width, UNIT_ROWS)])
    ]
    copies[0].start()
    pooled = a_ref[...]
    wide = jnp.dot(pooled, full[0:width, :], preferred_element_type=F32).reshape(slots, heads, width)
    context = jnp.sum(wide * head_mask(heads, width)[None], axis=1)
    inv = lax.rsqrt(jnp.sum(context * context, axis=-1, keepdims=True) + epsilon)
    unit = context * inv
    kept = terms(unit) + terms(jnp.broadcast_to(inv, unit.shape))
    full[width:, :] = jnp.concatenate(kept, axis=0).astype(BF16)
    copies[1].start()
    wide_pooled = pooled.astype(F32)
    for p in range(shards):
        moved = jnp.concatenate(
            [
                wide_pooled[b * heads : (b + 1) * heads, p * cut : (p + 1) * cut]
                for b in range(slots)
            ],
            axis=1,
        )
        out_ref[p] = jnp.concatenate([moved, unit], axis=0).astype(BF16)
    for copy in copies:
        copy.wait()


def caption_body(caption_ref, unit_ref, inv_ref, text_ref):
    caption = caption_ref[...].astype(F32)
    inv = lax.rsqrt(jnp.sum(caption * caption, axis=-1, keepdims=True) + epsilon)
    unit = caption * inv
    unit_ref[...] = unit
    inv_ref[...] = jnp.broadcast_to(inv, inv_ref.shape)
    text_ref[...] = unit.astype(BF16)


def pair_body(place, scalars, got_ref, text_ref, d_image_ref, coefficient_ref, image_ref, loss_ref):
    loaders, got_rows, width = got_ref.shape
    slots = d_image_ref.shape[1]
    images = jnp.concatenate(
        [got_ref[s].astype(F32)[got_rows - slots :] for s in range(loaders)], axis=0
    ).astype(BF16)
    image_ref[...] = images
    texts = text_ref[...]
    count = images.shape[0]
    text_count = texts.shape[0]
    scale = scalars[0]
    logits = scale * nt_dot(images, texts) + scalars[1]
    row = lax.broadcasted_iota(jnp.int32, (count, text_count), 0)
    column = lax.broadcasted_iota(jnp.int32, (count, text_count), 1)
    loader, owner = row // slots, row % slots
    matched = (owner == place[0]) & (column == loader)
    matched = matched.astype(F32)
    decay = jnp.exp(-jnp.abs(logits))
    signed = (1.0 - 2.0 * matched) * logits
    losses = jnp.maximum(signed, 0.0) + jnp.log1p(decay)
    sigmoid = jnp.where(logits >= 0.0, 1.0, decay) / (1.0 + decay)
    coefficient = (scale * (sigmoid - matched)).astype(BF16)
    coefficient_ref[...] = coefficient
    d_image = jnp.dot(coefficient, texts, preferred_element_type=F32)
    d_image_ref[...] = d_image.reshape(d_image_ref.shape).astype(BF16)
    per_image = jnp.sum(losses, axis=-1, keepdims=True)
    per_owner = jnp.sum(per_image.reshape(loaders, slots, 1), axis=0)
    loss_ref[...] = jnp.broadcast_to(per_owner, loss_ref.shape)


def text_body(coefficient_ref, image_ref, keep_ref, send_ref):
    d_text = tn_dot(coefficient_ref[...], image_ref[...])
    half = keep_ref.shape[0]
    keep_ref[...] = d_text[:half]
    send_ref[...] = d_text[half:].astype(BF16)


def fold_body(total_ref, got_ref, keep_ref, send_ref):
    total = total_ref[...] + got_ref[...].astype(F32)
    half = keep_ref.shape[0]
    keep_ref[...] = total[:half]
    send_ref[...] = total[half:].astype(BF16)


def split_body(total_ref, got_ref, keep_ref, *block_refs):
    total = total_ref[...] + got_ref[...].astype(F32)
    rows = keep_ref.shape[0]
    keep_ref[...] = total[:rows]
    for k, block_ref in enumerate(block_refs):
        block_ref[...] = total[(k + 1) * rows : (k + 2) * rows].astype(BF16)


def back_body(
    owners, got_in, full_in, x_in, side_in, const_in, loss_in, out_ref,
    got_ref, full, x_ref, side_ref, const_ref, loss_ref, normed_ref, scaled_ref, right, result, sems,
):
    slots, rows, width = x_ref.shape
    lanes = side_ref.shape[1] // 2
    heads = lanes // slots
    cut = width // slots
    scale = 1.0 / math.sqrt(width // heads)
    chunk = width // 3
    rows_of = [pl.ds(width, UNIT_ROWS)] + [pl.ds(c * chunk, chunk) for c in range(3)]
    pairs = [
        (full_in.at[rows_of[0], :], full.at[rows_of[0], :]),
        (got_in, got_ref),
        (side_in, side_ref),
        (const_in, const_ref),
        (x_in.at[0], x_ref),
    ]
    pairs += [(full_in.at[at, :], full.at[at, :]) for at in rows_of[1:]]
    pairs += [(loss_in, loss_ref)]
    copies = [
        pltpu.make_async_copy(source, target, sems.at[k]) for k, (source, target) in enumerate(pairs)
    ]
    for copy in copies:
        copy.start()
    copies[0].wait()
    copies[1].wait()
    d_image = jnp.sum(got_ref[...].astype(F32), axis=0)
    kept = full[width:, :].astype(F32)
    unit = kept[0:slots] + kept[slots : 2 * slots] + kept[2 * slots : 3 * slots]
    inv_norm = kept[3 * slots : 4 * slots] + kept[4 * slots : 5 * slots] + kept[5 * slots :]
    along = jnp.sum(d_image * unit, axis=-1, keepdims=True)
    d_context = (d_image - unit * along) * inv_norm
    d_context = d_context.astype(BF16).astype(F32)
    spread = (d_context[:, None, :] * head_mask(heads, width)[None]).reshape(lanes, width).astype(BF16)
    copies[2].wait()
    copies[3].wait()
    gain = const_ref[heads : heads + 1, :]
    right[lanes:, :] = jnp.concatenate([const_ref[0:heads, :]] * slots, axis=0).astype(BF16)
    copies[4].wait()
    for r in range(slots):
        at = slice(r * rows, (r + 1) * rows)
        x = x_ref[source_of(owners, r, slots)].astype(F32)
        normed = (x - side_ref[at, 0:1]) * side_ref[at, lanes // 2 : lanes // 2 + 1]
        normed_ref[at, :] = normed
        scaled_ref[at, :] = (normed * gain).astype(BF16)
    for c in range(3):
        copies[5 + c].wait()
        at = slice(c * chunk, (c + 1) * chunk)
        right[0:lanes, at] = nt_dot(spread, full[at, :]).astype(BF16)
    scaled = scaled_ref[...]
    weights = side_ref[:, lanes:]
    d_weights = nt_dot(scaled, right[0:lanes, :])
    centre = jnp.sum(weights * d_weights, axis=0, keepdims=True)
    d_scores = (weights * (d_weights - centre) * scale).astype(BF16)
    left = jnp.concatenate([weights.astype(BF16), d_scores], axis=1)
    gain_total = jnp.zeros((8, width), F32)
    sent = []
    half = slots // 2
    for g in range(2):
        d_scaled_half = jnp.dot(
            left[g * half * rows : (g + 1) * half * rows], right[...], preferred_element_type=F32
        )
        for k in range(half):
            r = g * half + k
            at = slice(r * rows, (r + 1) * rows)
            d_scaled = d_scaled_half[k * rows : (k + 1) * rows]
            normed = normed_ref[at, :]
            product = d_scaled * normed
            gain_total = gain_total + jnp.sum(product.reshape(rows // 8, 8, width), axis=0)
            grad_in = d_scaled * gain
            mean_a = jnp.sum(grad_in, axis=-1, keepdims=True) * (1.0 / width)
            mean_b = jnp.sum(product * gain, axis=-1, keepdims=True) * (1.0 / width)
            inv = side_ref[at, lanes // 2 : lanes // 2 + 1]
            result[r, 0:rows, :] = (inv * (grad_in - mean_a - normed * mean_b)).astype(BF16)
        at = pl.ds(g * half, half)
        copy = pltpu.make_async_copy(
            result.at[at, pl.ds(0, rows), :], out_ref.at[at, pl.ds(0, rows), :], sems.at[9 + g]
        )
        copy.start()
        sent.append(copy)
    probe_total = jnp.sum(tn_dot(d_scores, scaled).reshape(slots, heads, width), axis=0)
    gain_sum = jnp.sum(gain_total, axis=0, keepdims=True)
    copies[8].wait()
    high, middle, low = terms(loss_ref[...])
    pad = jnp.zeros((8, 256 - cut), F32)
    for p in range(slots):
        at = slice(p * cut, (p + 1) * cut)
        losses = jnp.concatenate(
            [high[p : p + 1], middle[p : p + 1], low[p : p + 1], jnp.zeros((5, 128), F32)], axis=0
        )
        misc = jnp.concatenate(
            [
                probe_total[0:8, at],
                pad,
                probe_total[8:16, at],
                pad,
                jnp.broadcast_to(gain_sum[:, at], (8, cut)),
                pad,
                losses,
                jnp.zeros((8, width - 896), F32),
            ],
            axis=1,
        )
        result[p, rows : rows + 16, :] = jnp.concatenate([d_context, misc], axis=0).astype(BF16)
    tail = pl.ds(rows, 16)
    copy = pltpu.make_async_copy(
        result.at[:, tail, :], out_ref.at[:, tail, :], sems.at[11]
    )
    copy.start()
    for copy in sent + [copy]:
        copy.wait()


def last_body(got_ref, a_ref, row_ref, value_ref, probe_ref, gain_ref, loss_ref, tail, sems, *, texts):
    loaders, got_rows, width = got_ref.shape
    rows = row_ref.shape[2]
    heads, images, cut = a_ref.shape
    head_width = width // heads
    first = pltpu.make_async_copy(got_ref.at[:, pl.ds(rows, 16), :], tail, sems.at[0])
    first.start()
    second = pltpu.make_async_copy(got_ref.at[:, pl.ds(0, rows), :], row_ref.at[0], sems.at[1])
    second.start()
    first.wait()
    tails = [tail[s].astype(F32) for s in range(loaders)]
    d_context = jnp.concatenate([t[0:8] for t in tails], axis=0)
    mask = head_mask(heads, width)
    tiles = [None] * (width // 128)
    for h in range(heads):
        low, high = h * head_width // 128, -(-(h + 1) * head_width // 128)
        lanes = slice(low * 128, high * 128)
        part = tn_dot(a_ref[h], (d_context[:, lanes] * mask[h : h + 1, lanes]).astype(BF16))
        for t in range(low, high):
            piece = part[:, (t - low) * 128 : (t - low + 1) * 128]
            tiles[t] = piece if tiles[t] is None else tiles[t] + piece
    value_ref[0] = jnp.concatenate(tiles, axis=1).astype(BF16)
    misc = tails[0][8:16]
    for s in range(1, loaders):
        misc = misc + tails[s][8:16]
    probe_ref[...] = jnp.concatenate([misc[:, 0:cut], misc[:, 256 : 256 + cut]], axis=0).astype(BF16)
    gain_ref[...] = misc[0:1, 512 : 512 + cut].astype(BF16)
    loss_ref[...] = (misc[0:1, 768:769] + misc[1:2, 768:769] + misc[2:3, 768:769]) / texts
    second.wait()


def local(
    patches, counts, owners, captions, norm_gain, key_probe, value_weight, logit_scale, logit_bias
):
    _, slots, rows, width = patches.shape
    heads = key_probe.shape[1]
    peers = lax.axis_size("fsdp")
    ranks = lax.axis_size("dp")
    cut = width // peers
    core = lax.axis_index("dp") % 2
    place = lax.axis_index("fsdp").astype(jnp.int32).reshape(1)
    scalars = jnp.concatenate([logit_scale, logit_bias])
    gain = norm_gain.reshape(1, width)
    probe = key_probe.T
    shape = jax.ShapeDtypeStruct
    dma = pltpu.SemaphoreType.DMA

    start = core * (cut - SEND_ROWS)
    part = lax.dynamic_slice_in_dim(value_weight, start, SEND_ROWS, axis=0)
    mine = lax.all_to_all(
        jnp.broadcast_to(part[None], (peers, SEND_ROWS, width)), "fsdp", 0, 0, tiled=True
    )

    lanes = slots * heads
    side, pooled = call(
        pool_body,
        [
            (shape((slots * rows, 2 * lanes), F32), vspec()),
            (shape((lanes, width), BF16), vspec()),
        ],
        [sspec(), sspec(), vspec(), vspec(), vspec()],
        40_000_000,
        4_000_000,
        [pltpu.VMEM((slots * rows, width), BF16)],
        name="pool",
    )(owners[0], counts[0], patches[0], gain, probe)

    caption_unit, caption_inv, texts = call(
        caption_body,
        [
            (shape((slots, width), F32), vspec()),
            (shape((slots, 128), F32), vspec()),
            (shape((slots, width), BF16), vspec()),
        ],
        [vspec()],
        40_000_000,
        4_000_000,
        name="caption",
    )(captions[0])
    if ranks > 2:
        for bit in (8, 4, 2):
            texts = jnp.concatenate([texts, swapped(texts, bit)], axis=0)
    mine, texts, pooled = lax.optimization_barrier((mine, texts, pooled))
    other = swapped(mine, 1)
    if ranks > 2:
        flank = swapped(texts, SIDE_BIT)
    full, sent = call(
        image_body,
        [
            (shape((STASH_ROWS, width), BF16), hspec()),
            (shape((peers, heads + slots, width), BF16), vspec()),
        ],
        [vspec()] * 3,
        400_000_000,
        6_000_000,
        [pltpu.VMEM((width + UNIT_ROWS, width), BF16), dma((2,))],
        name="image",
        limit=VMEM_IMAGE,
    )(mine, other, pooled)
    if ranks > 2:
        full, flank = lax.optimization_barrier((full, flank))
        texts = jnp.concatenate([texts, flank], axis=0)
    got = lax.all_to_all(sent, "fsdp", 0, 0, tiled=True)
    texts = jnp.concatenate([texts, swapped(texts, CORE_BIT)], axis=0)
    count = peers * slots
    text_count = ranks * slots
    d_image_part, coefficient, images, loss_sums = call(
        pair_body,
        [
            (shape((peers, slots, width), BF16), vspec()),
            (shape((count, text_count), BF16), vspec()),
            (shape((count, width), BF16), vspec()),
            (shape((slots, 128), F32), vspec()),
        ],
        [sspec(), sspec(), vspec(), vspec()],
        80_000_000,
        2_000_000,
        name="pair",
    )(place, scalars, got, texts)
    d_image_got = lax.all_to_all(d_image_part, "fsdp", 0, 0, tiled=True)

    def halves(rows_out):
        return [
            (shape((rows_out, width), F32), vspec()),
            (shape((rows_out, width), BF16), vspec()),
        ]

    def fold(keep, send, bit):
        if bit >= ranks:
            return keep, send
        return call(
            fold_body, halves(keep.shape[0] // 2), [vspec(), vspec()], 40_000_000, 1_000_000, name="fold"
        )(keep, swapped(send, bit))

    keep, send = call(
        text_body, halves(text_count // 2), [vspec(), vspec()], 0, 0, name="text"
    )(coefficient, images)
    if ranks > 2:
        keep, send = fold(keep, send, CORE_BIT)
    if ranks > 2:
        keep, send = fold(keep, send, SIDE_BIT)

    const = jnp.concatenate([probe.astype(F32), jnp.broadcast_to(gain, (8, width))], axis=0)
    outgoing = call(
        back_body,
        [(shape((peers, rows + 16, width), BF16), hspec())],
        [sspec()] + [hspec()] * 6,
        500_000_000,
        8_000_000,
        [
            pltpu.VMEM((peers, slots, width), BF16),
            pltpu.VMEM((width + UNIT_ROWS, width), BF16),
            pltpu.VMEM((slots, rows, width), BF16),
            pltpu.VMEM((slots * rows, 2 * lanes), F32),
            pltpu.VMEM((heads + 8, width), F32),
            pltpu.VMEM((slots, 128), F32),
            pltpu.VMEM((slots * rows, width), F32),
            pltpu.VMEM((slots * rows, width), BF16),
            pltpu.VMEM((2 * lanes, width), BF16),
            pltpu.VMEM((peers, rows + 16, width), BF16),
            dma((12,)),
        ],
        name="back",
        limit=VMEM_LARGE,
    )(owners[0], d_image_got, full, patches, side, const, loss_sums)[0]
    outgoing, keep, send = lax.optimization_barrier((outgoing, keep, send))
    arrived = lax.all_to_all(outgoing, "fsdp", 0, 0, tiled=True)
    if ranks > 2:
        d_caption, *blocks = call(
            split_body,
            [(shape((slots, width), F32), vspec())] + [(shape((slots, width), BF16), vspec())] * 3,
            [vspec(), vspec()],
            40_000_000,
            1_000_000,
            name="split",
        )(keep, swapped(send, NEXT_BIT))
        blocks = [swapped(block, bit) for block, bit in zip(blocks, Z_BITS)]
    else:
        d_caption, blocks = keep, [swapped(send, CORE_BIT)]

    pooled_got = (
        got[:, :heads]
        .reshape(peers, heads, slots, cut)
        .transpose(1, 0, 2, 3)
        .reshape(heads, peers * slots, cut)
    )
    batch = ranks * peers * slots

    def last(*refs):
        last_body(*refs, texts=batch)

    row_grad, value_grad, probe_t, gain_grad, loss_part = call(
        last,
        [
            (shape((1, slots, rows, width), BF16), hspec()),
            (shape((1, cut, width), BF16), vspec()),
            (shape((heads, cut), BF16), vspec()),
            (shape((1, cut), BF16), vspec()),
            (shape((1, 1), F32), vspec()),
        ],
        [hspec(), vspec()],
        400_000_000,
        3_000_000,
        [pltpu.VMEM((peers, 16, width), BF16), dma((2,))],
        name="last",
    )(arrived, pooled_got)

    loss_part, blocks = lax.optimization_barrier((loss_part, blocks))
    for block in blocks:
        d_caption = d_caption + block.astype(F32)
    text_grad = (
        (d_caption - caption_unit * jnp.sum(d_caption * caption_unit, axis=-1, keepdims=True))
        * caption_inv[:, 0:1]
    ).astype(BF16)
    return (loss_part, row_grad, text_grad[None], value_grad, probe_t.T[None], gain_grad)


def solution(mesh):
    placed = (
        P(("dp", "fsdp"), None, None, None),
        P(("dp", "fsdp"), None),
        P(("dp", "fsdp"), None),
        P(("dp", "fsdp"), None, None),
        P(),
        P(),
        P("fsdp", None),
        P(),
        P(),
    )
    return jax.shard_map(
        local,
        mesh=mesh,
        in_specs=placed,
        out_specs=(
            P("dp", "fsdp"),
            P(("dp", "fsdp"), None, None, None),
            P(("dp", "fsdp"), None, None),
            P("dp", "fsdp", None),
            P("dp", "fsdp", None),
            P("dp", "fsdp"),
        ),
        check_vma=False,
    )
```

```python
import math

import jax
import jax.numpy as jnp
from jax import lax
from jax.experimental import pallas as pl
from jax.experimental.pallas import tpu as pltpu
from jax.sharding import PartitionSpec as P

epsilon = 1e-06
F32 = jnp.float32
BF16 = jnp.bfloat16

VMEM_LIMIT = 16 * 1024 * 1024
VMEM_LARGE = 60_000_000
VMEM_IMAGE = 28_000_000
KEPT_ROWS = 96
STASH_ROWS = 15_616
SEND_ROWS = 72


Z_BITS = (8, 4, 12)
NEXT_BIT, SIDE_BIT, CORE_BIT = 2, 16, 1


def swapped(block, bit):
    return lax.ppermute(block, "dp", [(i, i ^ bit) for i in range(lax.axis_size("dp"))])


def vspec():
    return pl.BlockSpec(memory_space=pltpu.VMEM)


def sspec():
    return pl.BlockSpec(memory_space=pltpu.SMEM)


def hspec():
    return pl.BlockSpec(memory_space=pltpu.HBM)


def call(body, outs, in_specs, flops, nbytes, scratch=(), name=None, limit=VMEM_LIMIT):
    return pl.pallas_call(
        body,
        out_shape=[shape for shape, _ in outs],
        in_specs=in_specs,
        out_specs=[spec for _, spec in outs],
        scratch_shapes=list(scratch),
        compiler_params=pltpu.CompilerParams(vmem_limit_bytes=limit),
        cost_estimate=pl.CostEstimate(flops=flops, bytes_accessed=nbytes, transcendentals=0),
        name=name,
    )


def source_of(owners, owner, slots):
    source = jnp.int32(0)
    for k in range(slots):
        source = source + jnp.where(owners[k] == owner, k, 0)
    return source


def nt_dot(a, b):
    return lax.dot_general(a, b, (((1,), (1,)), ((), ())), preferred_element_type=F32)


def tn_dot(a, b):
    return lax.dot_general(a, b, (((0,), (0,)), ((), ())), preferred_element_type=F32)


def terms(value):
    high = value.astype(BF16).astype(F32)
    middle = (value - high).astype(BF16).astype(F32)
    return [high, middle, value - high - middle]


def head_mask(heads, width):
    head_width = width // heads
    low = lax.broadcasted_iota(jnp.int32, (heads, width), 0) * head_width
    column = lax.broadcasted_iota(jnp.int32, (heads, width), 1)
    return ((column >= low) & (column < low + head_width)).astype(F32)


def pool_body(owners, counts, x_ref, gain_ref, probe_ref, side_ref, a_ref, scaled_ref):
    slots, rows, width = x_ref.shape
    heads = probe_ref.shape[0]
    scale = 1.0 / math.sqrt(width // heads)
    gain = gain_ref[...]
    lanes = slots * heads
    column = lax.broadcasted_iota(jnp.int32, (rows, lanes), 1)
    patch = lax.broadcasted_iota(jnp.int32, (rows, lanes), 0)
    masks = []
    for r in range(slots):
        source = source_of(owners, r, slots)
        x = x_ref[source].astype(F32)
        mean = jnp.sum(x, axis=-1, keepdims=True) * (1.0 / width)
        centered = x - mean
        var = jnp.sum(centered * centered, axis=-1, keepdims=True) * (1.0 / width)
        inv = lax.rsqrt(var + epsilon)
        scaled_ref[r * rows : (r + 1) * rows, :] = ((centered * inv) * gain).astype(BF16)
        side_ref[r * rows : (r + 1) * rows, 0:lanes] = jnp.where(column < lanes // 2, mean, inv)
        own = (column >= r * heads) & (column < (r + 1) * heads)
        masks.append(jnp.where(own & (patch < counts[source]), 1.0, 0.0))
    valid = jnp.concatenate(masks, axis=0) > 0.5
    scaled = scaled_ref[...]
    tiled = jnp.concatenate([probe_ref[...].astype(F32)] * slots, axis=0).astype(BF16)
    scores = nt_dot(scaled, tiled) * scale
    highest = jnp.max(jnp.where(valid, scores, -jnp.inf), axis=0, keepdims=True)
    raised = jnp.where(valid, jnp.exp(jnp.where(valid, scores - highest, 0.0)), 0.0)
    weights = raised / jnp.sum(raised, axis=0, keepdims=True)
    side_ref[:, lanes:] = weights
    a_ref[...] = tn_dot(weights.astype(BF16), scaled).astype(BF16)


def image_body(
    mine_ref, other_ref, a_ref, gain_ref, probe_ref, full_out, out_ref, full, sems
):
    shards, part_rows, width = mine_ref.shape
    slots = shards
    heads = a_ref.shape[0] // slots
    cut = width // shards
    rest = cut - part_rows
    core = lax.rem(lax.axis_index("dp"), 2)

    def put(low_ref, high_ref):
        for j in range(shards):
            full[j * cut : j * cut + part_rows, :] = low_ref[j]
            full[j * cut + part_rows : (j + 1) * cut, :] = high_ref[j, part_rows - rest :, :]

    @pl.when(core == 0)
    def _():
        put(mine_ref, other_ref)

    @pl.when(core != 0)
    def _():
        put(other_ref, mine_ref)

    copies = [
        pltpu.make_async_copy(full.at[at, :], full_out.at[at, :], sems.at[k])
        for k, at in enumerate([pl.ds(0, width), pl.ds(width, KEPT_ROWS)])
    ]
    copies[0].start()
    pooled = a_ref[...]
    wide = jnp.dot(pooled, full[0:width, :], preferred_element_type=F32).reshape(slots, heads, width)
    context = jnp.sum(wide * head_mask(heads, width)[None], axis=1)
    inv = lax.rsqrt(jnp.sum(context * context, axis=-1, keepdims=True) + epsilon)
    unit = context * inv
    kept = terms(unit) + terms(jnp.broadcast_to(inv, unit.shape))
    kept += terms(jnp.broadcast_to(gain_ref[...], unit.shape)) + [jnp.zeros_like(unit)]
    kept += [probe_ref[...].astype(F32)]
    full[width:, :] = jnp.concatenate(kept, axis=0).astype(BF16)
    copies[1].start()
    wide_pooled = pooled.astype(F32)
    for p in range(shards):
        moved = jnp.concatenate(
            [
                wide_pooled[b * heads : (b + 1) * heads, p * cut : (p + 1) * cut]
                for b in range(slots)
            ],
            axis=1,
        )
        out_ref[p] = jnp.concatenate([moved, unit], axis=0).astype(BF16)
    for copy in copies:
        copy.wait()


def caption_body(caption_ref, unit_ref, inv_ref, text_ref):
    caption = caption_ref[...].astype(F32)
    inv = lax.rsqrt(jnp.sum(caption * caption, axis=-1, keepdims=True) + epsilon)
    unit = caption * inv
    unit_ref[...] = unit
    inv_ref[...] = jnp.broadcast_to(inv, inv_ref.shape)
    text_ref[...] = unit.astype(BF16)


def pair_body(place, scalars, got_ref, text_ref, d_image_ref, coefficient_ref, image_ref, loss_ref):
    loaders, got_rows, width = got_ref.shape
    slots = d_image_ref.shape[1]
    images = jnp.concatenate(
        [got_ref[s].astype(F32)[got_rows - slots :] for s in range(loaders)], axis=0
    ).astype(BF16)
    image_ref[...] = images
    texts = text_ref[...]
    count = images.shape[0]
    text_count = texts.shape[0]
    scale = scalars[0]
    logits = scale * nt_dot(images, texts) + scalars[1]
    row = lax.broadcasted_iota(jnp.int32, (count, text_count), 0)
    column = lax.broadcasted_iota(jnp.int32, (count, text_count), 1)
    loader, owner = row // slots, row % slots
    matched = (owner == place[0]) & (column == loader)
    matched = matched.astype(F32)
    decay = jnp.exp(-jnp.abs(logits))
    signed = (1.0 - 2.0 * matched) * logits
    losses = jnp.maximum(signed, 0.0) + jnp.log1p(decay)
    sigmoid = jnp.where(logits >= 0.0, 1.0, decay) / (1.0 + decay)
    coefficient = (scale * (sigmoid - matched)).astype(BF16)
    coefficient_ref[...] = coefficient
    d_image = jnp.dot(coefficient, texts, preferred_element_type=F32)
    d_image_ref[...] = d_image.reshape(d_image_ref.shape).astype(BF16)
    per_image = jnp.sum(losses, axis=-1, keepdims=True)
    per_owner = jnp.sum(per_image.reshape(loaders, slots, 1), axis=0)
    loss_ref[...] = jnp.broadcast_to(per_owner, loss_ref.shape)


def text_body(coefficient_ref, image_ref, keep_ref, send_ref):
    d_text = tn_dot(coefficient_ref[...], image_ref[...])
    half = keep_ref.shape[0]
    keep_ref[...] = d_text[:half]
    send_ref[...] = d_text[half:].astype(BF16)


def fold_body(total_ref, got_ref, keep_ref, send_ref):
    total = total_ref[...] + got_ref[...].astype(F32)
    half = keep_ref.shape[0]
    keep_ref[...] = total[:half]
    send_ref[...] = total[half:].astype(BF16)


def split_body(total_ref, got_ref, keep_ref, *block_refs):
    total = total_ref[...] + got_ref[...].astype(F32)
    rows = keep_ref.shape[0]
    keep_ref[...] = total[:rows]
    for k, block_ref in enumerate(block_refs):
        block_ref[...] = total[(k + 1) * rows : (k + 2) * rows].astype(BF16)


def finish_body(total_ref, unit_ref, inv_ref, *refs):
    d_caption = total_ref[...]
    for block_ref in refs[:-1]:
        d_caption = d_caption + block_ref[...].astype(F32)
    unit = unit_ref[...]
    along = jnp.sum(d_caption * unit, axis=-1, keepdims=True)
    refs[-1][...] = ((d_caption - unit * along) * inv_ref[:, 0:1]).astype(BF16)


def back_body(
    owners_in, got_in, full_in, x_in, side_in, loss_in, out_ref,
    owners, got_ref, full, x_ref, side_ref, loss_ref, normed_ref, scaled_ref, right, result, sems,
):
    slots, rows, width = x_ref.shape
    lanes = side_ref.shape[1] // 2
    heads = lanes // slots
    cut = width // slots
    scale = 1.0 / math.sqrt(width // heads)
    chunk = width // 3
    rows_of = [pl.ds(width, KEPT_ROWS)] + [pl.ds(c * chunk, chunk) for c in range(3)]
    pairs = [
        (full_in.at[rows_of[0], :], full.at[rows_of[0], :]),
        (got_in, got_ref),
        (owners_in, owners),
        (side_in, side_ref),
        (x_in.at[0], x_ref),
    ]
    pairs += [(full_in.at[at, :], full.at[at, :]) for at in rows_of[1:]]
    pairs += [(loss_in, loss_ref)]
    copies = [
        pltpu.make_async_copy(source, target, sems.at[k]) for k, (source, target) in enumerate(pairs)
    ]
    for copy in copies:
        copy.start()
    copies[0].wait()
    copies[1].wait()
    d_image = jnp.sum(got_ref[...].astype(F32), axis=0)
    kept = full[width:, :].astype(F32)

    def whole(first):
        return kept[first : first + 8] + kept[first + 8 : first + 16] + kept[first + 16 : first + 24]

    unit, inv_norm, gain = whole(0), whole(24), whole(48)[0:1]
    along = jnp.sum(d_image * unit, axis=-1, keepdims=True)
    d_context = (d_image - unit * along) * inv_norm
    d_context = d_context.astype(BF16).astype(F32)
    right[lanes:, :] = jnp.concatenate([kept[80 : 80 + heads]] * slots, axis=0).astype(BF16)
    spread = (d_context[:, None, :] * head_mask(heads, width)[None]).reshape(lanes, width).astype(BF16)
    copies[2].wait()
    copies[3].wait()
    copies[4].wait()
    for r in range(slots):
        at = slice(r * rows, (r + 1) * rows)
        x = x_ref[source_of(owners, r, slots)].astype(F32)
        normed = (x - side_ref[at, 0:1]) * side_ref[at, lanes // 2 : lanes // 2 + 1]
        normed_ref[at, :] = normed
        scaled_ref[at, :] = (normed * gain).astype(BF16)
    for c in range(3):
        copies[5 + c].wait()
        at = slice(c * chunk, (c + 1) * chunk)
        right[0:lanes, at] = nt_dot(spread, full[at, :]).astype(BF16)
    scaled = scaled_ref[...]
    weights = side_ref[:, lanes:]
    d_weights = nt_dot(scaled, right[0:lanes, :])
    centre = jnp.sum(weights * d_weights, axis=0, keepdims=True)
    d_scores = (weights * (d_weights - centre) * scale).astype(BF16)
    left = jnp.concatenate([weights.astype(BF16), d_scores], axis=1)
    gain_total = jnp.zeros((8, width), F32)
    sent = []
    half = slots // 2
    for g in range(2):
        d_scaled_half = jnp.dot(
            left[g * half * rows : (g + 1) * half * rows], right[...], preferred_element_type=F32
        )
        for k in range(half):
            r = g * half + k
            at = slice(r * rows, (r + 1) * rows)
            d_scaled = d_scaled_half[k * rows : (k + 1) * rows]
            normed = normed_ref[at, :]
            product = d_scaled * normed
            gain_total = gain_total + jnp.sum(product.reshape(rows // 8, 8, width), axis=0)
            grad_in = d_scaled * gain
            mean_a = jnp.sum(grad_in, axis=-1, keepdims=True) * (1.0 / width)
            mean_b = jnp.sum(product * gain, axis=-1, keepdims=True) * (1.0 / width)
            inv = side_ref[at, lanes // 2 : lanes // 2 + 1]
            result[r, 0:rows, :] = (inv * (grad_in - mean_a - normed * mean_b)).astype(BF16)
        at = pl.ds(g * half, half)
        copy = pltpu.make_async_copy(
            result.at[at, pl.ds(0, rows), :], out_ref.at[at, pl.ds(0, rows), :], sems.at[9 + g]
        )
        copy.start()
        sent.append(copy)
    probe_total = jnp.sum(tn_dot(d_scores, scaled).reshape(slots, heads, width), axis=0)
    gain_sum = jnp.sum(gain_total, axis=0, keepdims=True)
    copies[8].wait()
    high, middle, low = terms(loss_ref[...])
    pad = jnp.zeros((8, 256 - cut), F32)
    for p in range(slots):
        at = slice(p * cut, (p + 1) * cut)
        losses = jnp.concatenate(
            [high[p : p + 1], middle[p : p + 1], low[p : p + 1], jnp.zeros((5, 128), F32)], axis=0
        )
        misc = jnp.concatenate(
            [
                probe_total[0:8, at],
                pad,
                probe_total[8:16, at],
                pad,
                jnp.broadcast_to(gain_sum[:, at], (8, cut)),
                pad,
                losses,
                jnp.zeros((8, width - 896), F32),
            ],
            axis=1,
        )
        result[p, rows : rows + 16, :] = jnp.concatenate([d_context, misc], axis=0).astype(BF16)
    tail = pl.ds(rows, 16)
    copy = pltpu.make_async_copy(
        result.at[:, tail, :], out_ref.at[:, tail, :], sems.at[11]
    )
    copy.start()
    for copy in sent + [copy]:
        copy.wait()


def last_body(got_ref, a_ref, row_ref, value_ref, probe_ref, gain_ref, loss_ref, tail, sems, *, texts):
    loaders, got_rows, width = got_ref.shape
    rows = row_ref.shape[2]
    heads, images, cut = a_ref.shape
    head_width = width // heads
    first = pltpu.make_async_copy(got_ref.at[:, pl.ds(rows, 16), :], tail, sems.at[0])
    first.start()
    second = pltpu.make_async_copy(got_ref.at[:, pl.ds(0, rows), :], row_ref.at[0], sems.at[1])
    second.start()
    first.wait()
    tails = [tail[s].astype(F32) for s in range(loaders)]
    d_context = jnp.concatenate([t[0:8] for t in tails], axis=0)
    mask = head_mask(heads, width)
    tiles = [None] * (width // 128)
    for h in range(heads):
        low, high = h * head_width // 128, -(-(h + 1) * head_width // 128)
        lanes = slice(low * 128, high * 128)
        part = tn_dot(a_ref[h], (d_context[:, lanes] * mask[h : h + 1, lanes]).astype(BF16))
        for t in range(low, high):
            piece = part[:, (t - low) * 128 : (t - low + 1) * 128]
            tiles[t] = piece if tiles[t] is None else tiles[t] + piece
    value_ref[0] = jnp.concatenate(tiles, axis=1).astype(BF16)
    misc = tails[0][8:16]
    for s in range(1, loaders):
        misc = misc + tails[s][8:16]
    probe_ref[...] = jnp.concatenate([misc[:, 0:cut], misc[:, 256 : 256 + cut]], axis=0).astype(BF16)
    gain_ref[...] = misc[0:1, 512 : 512 + cut].astype(BF16)
    loss_ref[...] = (misc[0:1, 768:769] + misc[1:2, 768:769] + misc[2:3, 768:769]) / texts
    second.wait()


def local(
    patches, counts, owners, captions, norm_gain, key_probe, value_weight, logit_scale, logit_bias
):
    _, slots, rows, width = patches.shape
    heads = key_probe.shape[1]
    peers = lax.axis_size("fsdp")
    ranks = lax.axis_size("dp")
    cut = width // peers
    core = lax.axis_index("dp") % 2
    place = lax.axis_index("fsdp").astype(jnp.int32).reshape(1)
    scalars = jnp.concatenate([logit_scale, logit_bias])
    gain = norm_gain.reshape(1, width)
    probe = key_probe.T
    shape = jax.ShapeDtypeStruct
    dma = pltpu.SemaphoreType.DMA

    start = core * (cut - SEND_ROWS)
    part = lax.dynamic_slice_in_dim(value_weight, start, SEND_ROWS, axis=0)
    mine = lax.all_to_all(
        jnp.broadcast_to(part[None], (peers, SEND_ROWS, width)), "fsdp", 0, 0, tiled=True
    )

    lanes = slots * heads
    side, pooled = call(
        pool_body,
        [
            (shape((slots * rows, 2 * lanes), F32), vspec()),
            (shape((lanes, width), BF16), vspec()),
        ],
        [sspec(), sspec(), vspec(), vspec(), vspec()],
        40_000_000,
        4_000_000,
        [pltpu.VMEM((slots * rows, width), BF16)],
        name="pool",
    )(owners[0], counts[0], patches[0], gain, probe)

    caption_unit, caption_inv, texts = call(
        caption_body,
        [
            (shape((slots, width), F32), vspec()),
            (shape((slots, 128), F32), vspec()),
            (shape((slots, width), BF16), vspec()),
        ],
        [vspec()],
        40_000_000,
        4_000_000,
        name="caption",
    )(captions[0])
    if ranks > 2:
        for bit in (8, 4, 2):
            texts = jnp.concatenate([texts, swapped(texts, bit)], axis=0)
    mine, texts, pooled = lax.optimization_barrier((mine, texts, pooled))
    other = swapped(mine, 1)
    bits = [bit for bit in (SIDE_BIT, CORE_BIT, SIDE_BIT + CORE_BIT) if bit < ranks]
    flanks = [swapped(texts, bit) for bit in bits]
    full, sent = call(
        image_body,
        [
            (shape((STASH_ROWS, width), BF16), hspec()),
            (shape((peers, heads + slots, width), BF16), vspec()),
        ],
        [vspec()] * 5,
        400_000_000,
        6_000_000,
        [pltpu.VMEM((width + KEPT_ROWS, width), BF16), dma((2,))],
        name="image",
        limit=VMEM_IMAGE,
    )(mine, other, pooled, gain, probe)
    full, flanks = lax.optimization_barrier((full, flanks))
    got = lax.all_to_all(sent, "fsdp", 0, 0, tiled=True)
    texts = jnp.concatenate([texts] + flanks, axis=0)
    count = peers * slots
    text_count = ranks * slots
    d_image_part, coefficient, images, loss_sums = call(
        pair_body,
        [
            (shape((peers, slots, width), BF16), vspec()),
            (shape((count, text_count), BF16), vspec()),
            (shape((count, width), BF16), vspec()),
            (shape((slots, 128), F32), vspec()),
        ],
        [sspec(), sspec(), vspec(), vspec()],
        80_000_000,
        2_000_000,
        name="pair",
    )(place, scalars, got, texts)
    d_image_got = lax.all_to_all(d_image_part, "fsdp", 0, 0, tiled=True)

    def halves(rows_out):
        return [
            (shape((rows_out, width), F32), vspec()),
            (shape((rows_out, width), BF16), vspec()),
        ]

    def fold(keep, send, bit):
        if bit >= ranks:
            return keep, send
        return call(
            fold_body, halves(keep.shape[0] // 2), [vspec(), vspec()], 40_000_000, 1_000_000, name="fold"
        )(keep, swapped(send, bit))

    keep, send = call(
        text_body, halves(text_count // 2), [vspec(), vspec()], 0, 0, name="text"
    )(coefficient, images)
    if ranks > 2:
        keep, send = fold(keep, send, CORE_BIT)
    if ranks > 2:
        keep, send = fold(keep, send, SIDE_BIT)

    outgoing = call(
        back_body,
        [(shape((peers, rows + 16, width), BF16), hspec())],
        [hspec()] * 6,
        500_000_000,
        8_000_000,
        [
            pltpu.SMEM((slots,), jnp.int32),
            pltpu.VMEM((peers, slots, width), BF16),
            pltpu.VMEM((width + KEPT_ROWS, width), BF16),
            pltpu.VMEM((slots, rows, width), BF16),
            pltpu.VMEM((slots * rows, 2 * lanes), F32),
            pltpu.VMEM((slots, 128), F32),
            pltpu.VMEM((slots * rows, width), F32),
            pltpu.VMEM((slots * rows, width), BF16),
            pltpu.VMEM((2 * lanes, width), BF16),
            pltpu.VMEM((peers, rows + 16, width), BF16),
            dma((12,)),
        ],
        name="back",
        limit=40_000_000,
    )(owners[0], d_image_got, full, patches, side, loss_sums)[0]
    outgoing, keep, send = lax.optimization_barrier((outgoing, keep, send))
    arrived = lax.all_to_all(outgoing, "fsdp", 0, 0, tiled=True)
    if ranks > 2:
        d_caption, *blocks = call(
            split_body,
            [(shape((slots, width), F32), vspec())] + [(shape((slots, width), BF16), vspec())] * 3,
            [vspec(), vspec()],
            40_000_000,
            1_000_000,
            name="split",
        )(keep, swapped(send, NEXT_BIT))
        blocks = [swapped(block, bit) for block, bit in zip(blocks, Z_BITS)]
    else:
        d_caption, blocks = keep, [swapped(send, CORE_BIT)]

    pooled_got = (
        got[:, :heads]
        .reshape(peers, heads, slots, cut)
        .transpose(1, 0, 2, 3)
        .reshape(heads, peers * slots, cut)
    )
    batch = ranks * peers * slots

    def last(*refs):
        last_body(*refs, texts=batch)

    row_grad, value_grad, probe_t, gain_grad, loss_part = call(
        last,
        [
            (shape((1, slots, rows, width), BF16), hspec()),
            (shape((1, cut, width), BF16), vspec()),
            (shape((heads, cut), BF16), vspec()),
            (shape((1, cut), BF16), vspec()),
            (shape((1, 1), F32), vspec()),
        ],
        [hspec(), vspec()],
        400_000_000,
        3_000_000,
        [pltpu.VMEM((peers, 16, width), BF16), dma((2,))],
        name="last",
    )(arrived, pooled_got)

    loss_part, blocks = lax.optimization_barrier((loss_part, blocks))
    text_grad = call(
        finish_body,
        [(shape((slots, width), BF16), vspec())],
        [vspec()] * (3 + len(blocks)),
        0,
        0,
        name="finish",
    )(d_caption, caption_unit, caption_inv, *blocks)[0]
    return (loss_part, row_grad, text_grad[None], value_grad, probe_t.T[None], gain_grad)


def solution(mesh):
    placed = (
        P(("dp", "fsdp"), None, None, None),
        P(("dp", "fsdp"), None),
        P(("dp", "fsdp"), None),
        P(("dp", "fsdp"), None, None),
        P(),
        P(),
        P("fsdp", None),
        P(),
        P(),
    )
    return jax.shard_map(
        local,
        mesh=mesh,
        in_specs=placed,
        out_specs=(
            P("dp", "fsdp"),
            P(("dp", "fsdp"), None, None, None),
            P(("dp", "fsdp"), None, None),
            P("dp", "fsdp", None),
            P("dp", "fsdp", None),
            P("dp", "fsdp"),
        ),
        check_vma=False,
    )
```

```python
import math

import jax
import jax.numpy as jnp
from jax import lax
from jax.experimental import pallas as pl
from jax.experimental.pallas import tpu as pltpu
from jax.sharding import PartitionSpec as P

epsilon = 1e-06
F32 = jnp.float32
BF16 = jnp.bfloat16

VMEM_LIMIT = 16 * 1024 * 1024
VMEM_LARGE = 60_000_000
VMEM_IMAGE = 28_000_000
KEPT_ROWS = 96
STASH_ROWS = 15_616
SEND_ROWS = 72


Z_BITS = (8, 4, 12)
NEXT_BIT, SIDE_BIT, CORE_BIT = 2, 16, 1


def swapped(block, bit):
    return lax.ppermute(block, "dp", [(i, i ^ bit) for i in range(lax.axis_size("dp"))])


def vspec():
    return pl.BlockSpec(memory_space=pltpu.VMEM)


def sspec():
    return pl.BlockSpec(memory_space=pltpu.SMEM)


def hspec():
    return pl.BlockSpec(memory_space=pltpu.HBM)


def call(body, outs, in_specs, flops, nbytes, scratch=(), name=None, limit=VMEM_LIMIT):
    return pl.pallas_call(
        body,
        out_shape=[shape for shape, _ in outs],
        in_specs=in_specs,
        out_specs=[spec for _, spec in outs],
        scratch_shapes=list(scratch),
        compiler_params=pltpu.CompilerParams(vmem_limit_bytes=limit),
        cost_estimate=pl.CostEstimate(flops=flops, bytes_accessed=nbytes, transcendentals=0),
        name=name,
    )


def source_of(owners, owner, slots):
    source = jnp.int32(0)
    for k in range(slots):
        source = source + jnp.where(owners[k] == owner, k, 0)
    return source


def nt_dot(a, b):
    return lax.dot_general(a, b, (((1,), (1,)), ((), ())), preferred_element_type=F32)


def tn_dot(a, b):
    return lax.dot_general(a, b, (((0,), (0,)), ((), ())), preferred_element_type=F32)


def terms(value):
    high = value.astype(BF16).astype(F32)
    middle = (value - high).astype(BF16).astype(F32)
    return [high, middle, value - high - middle]


def head_mask(heads, width):
    head_width = width // heads
    low = lax.broadcasted_iota(jnp.int32, (heads, width), 0) * head_width
    column = lax.broadcasted_iota(jnp.int32, (heads, width), 1)
    return ((column >= low) & (column < low + head_width)).astype(F32)


def pool_body(owners, counts, x_ref, gain_ref, probe_ref, side_ref, a_ref, scaled_ref):
    slots, rows, width = x_ref.shape
    heads = probe_ref.shape[0]
    scale = 1.0 / math.sqrt(width // heads)
    gain = gain_ref[...]
    lanes = slots * heads
    column = lax.broadcasted_iota(jnp.int32, (rows, lanes), 1)
    patch = lax.broadcasted_iota(jnp.int32, (rows, lanes), 0)
    masks = []
    for r in range(slots):
        source = source_of(owners, r, slots)
        x = x_ref[source].astype(F32)
        mean = jnp.sum(x, axis=-1, keepdims=True) * (1.0 / width)
        centered = x - mean
        var = jnp.sum(centered * centered, axis=-1, keepdims=True) * (1.0 / width)
        inv = lax.rsqrt(var + epsilon)
        scaled_ref[r * rows : (r + 1) * rows, :] = ((centered * inv) * gain).astype(BF16)
        side_ref[r * rows : (r + 1) * rows, 0:lanes] = jnp.where(column < lanes // 2, mean, inv)
        own = (column >= r * heads) & (column < (r + 1) * heads)
        masks.append(jnp.where(own & (patch < counts[source]), 1.0, 0.0))
    valid = jnp.concatenate(masks, axis=0) > 0.5
    scaled = scaled_ref[...]
    tiled = jnp.concatenate([probe_ref[...].astype(F32)] * slots, axis=0).astype(BF16)
    scores = nt_dot(scaled, tiled) * scale
    highest = jnp.max(jnp.where(valid, scores, -jnp.inf), axis=0, keepdims=True)
    raised = jnp.where(valid, jnp.exp(jnp.where(valid, scores - highest, 0.0)), 0.0)
    weights = raised / jnp.sum(raised, axis=0, keepdims=True)
    side_ref[:, lanes:] = weights
    a_ref[...] = tn_dot(weights.astype(BF16), scaled).astype(BF16)


def image_body(
    mine_ref, other_ref, a_ref, gain_ref, probe_ref, full_out, out_ref, full, sems
):
    shards, part_rows, width = mine_ref.shape
    slots = shards
    heads = a_ref.shape[0] // slots
    cut = width // shards
    rest = cut - part_rows
    core = lax.rem(lax.axis_index("dp"), 2)

    def put(low_ref, high_ref):
        for j in range(shards):
            full[j * cut : j * cut + part_rows, :] = low_ref[j]
            full[j * cut + part_rows : (j + 1) * cut, :] = high_ref[j, part_rows - rest :, :]

    @pl.when(core == 0)
    def _():
        put(mine_ref, other_ref)

    @pl.when(core != 0)
    def _():
        put(other_ref, mine_ref)

    copies = [
        pltpu.make_async_copy(full.at[at, :], full_out.at[at, :], sems.at[k])
        for k, at in enumerate([pl.ds(0, width), pl.ds(width, KEPT_ROWS)])
    ]
    copies[0].start()
    pooled = a_ref[...]
    wide = jnp.dot(pooled, full[0:width, :], preferred_element_type=F32).reshape(slots, heads, width)
    context = jnp.sum(wide * head_mask(heads, width)[None], axis=1)
    inv = lax.rsqrt(jnp.sum(context * context, axis=-1, keepdims=True) + epsilon)
    unit = context * inv
    kept = terms(unit) + terms(jnp.broadcast_to(inv, unit.shape))
    kept += terms(jnp.broadcast_to(gain_ref[...], unit.shape)) + [jnp.zeros_like(unit)]
    kept += [probe_ref[...].astype(F32)]
    full[width:, :] = jnp.concatenate(kept, axis=0).astype(BF16)
    copies[1].start()
    wide_pooled = pooled.astype(F32)
    for p in range(shards):
        moved = jnp.concatenate(
            [
                wide_pooled[b * heads : (b + 1) * heads, p * cut : (p + 1) * cut]
                for b in range(slots)
            ],
            axis=1,
        )
        out_ref[p] = jnp.concatenate([moved, unit], axis=0).astype(BF16)
    for copy in copies:
        copy.wait()


def caption_body(caption_ref, unit_ref, inv_ref, text_ref):
    caption = caption_ref[...].astype(F32)
    inv = lax.rsqrt(jnp.sum(caption * caption, axis=-1, keepdims=True) + epsilon)
    unit = caption * inv
    unit_ref[...] = unit
    inv_ref[...] = jnp.broadcast_to(inv, inv_ref.shape)
    text_ref[...] = unit.astype(BF16)


def pair_body(place, scalars, got_ref, text_ref, d_image_ref, keep_ref, send_ref, loss_ref):
    loaders, got_rows, width = got_ref.shape
    slots = d_image_ref.shape[1]
    images = jnp.concatenate(
        [got_ref[s].astype(F32)[got_rows - slots :] for s in range(loaders)], axis=0
    ).astype(BF16)
    texts = text_ref[...]
    count = images.shape[0]
    text_count = texts.shape[0]
    scale = scalars[0]
    logits = scale * nt_dot(images, texts) + scalars[1]
    row = lax.broadcasted_iota(jnp.int32, (count, text_count), 0)
    column = lax.broadcasted_iota(jnp.int32, (count, text_count), 1)
    loader, owner = row // slots, row % slots
    matched = (owner == place[0]) & (column == loader)
    matched = matched.astype(F32)
    decay = jnp.exp(-jnp.abs(logits))
    signed = (1.0 - 2.0 * matched) * logits
    losses = jnp.maximum(signed, 0.0) + jnp.log1p(decay)
    sigmoid = jnp.where(logits >= 0.0, 1.0, decay) / (1.0 + decay)
    coefficient = (scale * (sigmoid - matched)).astype(BF16)
    d_image = jnp.dot(coefficient, texts, preferred_element_type=F32)
    d_image_ref[...] = d_image.reshape(d_image_ref.shape).astype(BF16)
    d_text = tn_dot(coefficient, images)
    half = keep_ref.shape[0]
    keep_ref[...] = d_text[:half]
    send_ref[...] = d_text[half:].astype(BF16)
    per_image = jnp.sum(losses, axis=-1, keepdims=True)
    per_owner = jnp.sum(per_image.reshape(loaders, slots, 1), axis=0)
    loss_ref[...] = jnp.broadcast_to(per_owner, loss_ref.shape)


def fold_body(total_ref, got_ref, keep_ref, send_ref):
    total = total_ref[...] + got_ref[...].astype(F32)
    half = keep_ref.shape[0]
    keep_ref[...] = total[:half]
    send_ref[...] = total[half:].astype(BF16)


def split_body(total_ref, got_ref, keep_ref, *block_refs):
    total = total_ref[...] + got_ref[...].astype(F32)
    rows = keep_ref.shape[0]
    keep_ref[...] = total[:rows]
    for k, block_ref in enumerate(block_refs):
        block_ref[...] = total[(k + 1) * rows : (k + 2) * rows].astype(BF16)


def back_body(
    owners_in, got_in, full_in, x_in, side_in, loss_in, out_ref,
    owners, got_ref, full, x_ref, side_ref, loss_ref, normed_ref, scaled_ref, right, result, sems,
):
    slots, rows, width = x_ref.shape
    lanes = side_ref.shape[1] // 2
    heads = lanes // slots
    cut = width // slots
    scale = 1.0 / math.sqrt(width // heads)
    chunk = width // 3
    rows_of = [pl.ds(width, KEPT_ROWS)] + [pl.ds(c * chunk, chunk) for c in range(3)]
    pairs = [
        (full_in.at[rows_of[0], :], full.at[rows_of[0], :]),
        (got_in, got_ref),
        (owners_in, owners),
        (side_in, side_ref),
        (x_in.at[0], x_ref),
    ]
    pairs += [(full_in.at[at, :], full.at[at, :]) for at in rows_of[1:]]
    pairs += [(loss_in, loss_ref)]
    copies = [
        pltpu.make_async_copy(source, target, sems.at[k]) for k, (source, target) in enumerate(pairs)
    ]
    for copy in copies:
        copy.start()
    copies[0].wait()
    copies[1].wait()
    d_image = jnp.sum(got_ref[...].astype(F32), axis=0)
    kept = full[width:, :].astype(F32)

    def whole(first):
        return kept[first : first + 8] + kept[first + 8 : first + 16] + kept[first + 16 : first + 24]

    unit, inv_norm, gain = whole(0), whole(24), whole(48)[0:1]
    along = jnp.sum(d_image * unit, axis=-1, keepdims=True)
    d_context = (d_image - unit * along) * inv_norm
    d_context = d_context.astype(BF16).astype(F32)
    right[lanes:, :] = jnp.concatenate([kept[80 : 80 + heads]] * slots, axis=0).astype(BF16)
    spread = (d_context[:, None, :] * head_mask(heads, width)[None]).reshape(lanes, width).astype(BF16)
    copies[2].wait()
    copies[3].wait()
    copies[4].wait()
    for r in range(slots):
        at = slice(r * rows, (r + 1) * rows)
        x = x_ref[source_of(owners, r, slots)].astype(F32)
        normed = (x - side_ref[at, 0:1]) * side_ref[at, lanes // 2 : lanes // 2 + 1]
        normed_ref[at, :] = normed
        scaled_ref[at, :] = (normed * gain).astype(BF16)
    for c in range(3):
        copies[5 + c].wait()
        at = slice(c * chunk, (c + 1) * chunk)
        right[0:lanes, at] = nt_dot(spread, full[at, :]).astype(BF16)
    scaled = scaled_ref[...]
    weights = side_ref[:, lanes:]
    d_weights = nt_dot(scaled, right[0:lanes, :])
    centre = jnp.sum(weights * d_weights, axis=0, keepdims=True)
    d_scores = (weights * (d_weights - centre) * scale).astype(BF16)
    left = jnp.concatenate([weights.astype(BF16), d_scores], axis=1)
    gain_total = jnp.zeros((8, width), F32)
    sent = []
    half = slots // 2
    for g in range(2):
        d_scaled_half = jnp.dot(
            left[g * half * rows : (g + 1) * half * rows], right[...], preferred_element_type=F32
        )
        for k in range(half):
            r = g * half + k
            at = slice(r * rows, (r + 1) * rows)
            d_scaled = d_scaled_half[k * rows : (k + 1) * rows]
            normed = normed_ref[at, :]
            product = d_scaled * normed
            gain_total = gain_total + jnp.sum(product.reshape(rows // 8, 8, width), axis=0)
            grad_in = d_scaled * gain
            mean_a = jnp.sum(grad_in, axis=-1, keepdims=True) * (1.0 / width)
            mean_b = jnp.sum(product * gain, axis=-1, keepdims=True) * (1.0 / width)
            inv = side_ref[at, lanes // 2 : lanes // 2 + 1]
            result[r, 0:rows, :] = (inv * (grad_in - mean_a - normed * mean_b)).astype(BF16)
        at = pl.ds(g * half, half)
        copy = pltpu.make_async_copy(
            result.at[at, pl.ds(0, rows), :], out_ref.at[at, pl.ds(0, rows), :], sems.at[9 + g]
        )
        copy.start()
        sent.append(copy)
    probe_total = jnp.sum(tn_dot(d_scores, scaled).reshape(slots, heads, width), axis=0)
    gain_sum = jnp.sum(gain_total, axis=0, keepdims=True)
    copies[8].wait()
    high, middle, low = terms(loss_ref[...])
    pad = jnp.zeros((8, 256 - cut), F32)
    for p in range(slots):
        at = slice(p * cut, (p + 1) * cut)
        losses = jnp.concatenate(
            [high[p : p + 1], middle[p : p + 1], low[p : p + 1], jnp.zeros((5, 128), F32)], axis=0
        )
        misc = jnp.concatenate(
            [
                probe_total[0:8, at],
                pad,
                probe_total[8:16, at],
                pad,
                jnp.broadcast_to(gain_sum[:, at], (8, cut)),
                pad,
                losses,
                jnp.zeros((8, width - 896), F32),
            ],
            axis=1,
        )
        result[p, rows : rows + 16, :] = jnp.concatenate([d_context, misc], axis=0).astype(BF16)
    tail = pl.ds(rows, 16)
    copy = pltpu.make_async_copy(
        result.at[:, tail, :], out_ref.at[:, tail, :], sems.at[11]
    )
    copy.start()
    for copy in sent + [copy]:
        copy.wait()


def last_body(
    got_ref, a_ref, total_ref, unit_ref, inv_ref, *refs, blocks, texts
):
    row_ref, value_ref, probe_ref, gain_ref, loss_ref, text_ref, tail, sems = refs[blocks:]
    loaders, got_rows, width = got_ref.shape
    rows = row_ref.shape[2]
    heads, images, cut = a_ref.shape
    head_width = width // heads
    first = pltpu.make_async_copy(got_ref.at[:, pl.ds(rows, 16), :], tail, sems.at[0])
    first.start()
    second = pltpu.make_async_copy(got_ref.at[:, pl.ds(0, rows), :], row_ref.at[0], sems.at[1])
    second.start()
    first.wait()
    tails = [tail[s].astype(F32) for s in range(loaders)]
    d_context = jnp.concatenate([t[0:8] for t in tails], axis=0)
    mask = head_mask(heads, width)
    tiles = [None] * (width // 128)
    for h in range(heads):
        low, high = h * head_width // 128, -(-(h + 1) * head_width // 128)
        lanes = slice(low * 128, high * 128)
        part = tn_dot(a_ref[h], (d_context[:, lanes] * mask[h : h + 1, lanes]).astype(BF16))
        for t in range(low, high):
            piece = part[:, (t - low) * 128 : (t - low + 1) * 128]
            tiles[t] = piece if tiles[t] is None else tiles[t] + piece
    value_ref[0] = jnp.concatenate(tiles, axis=1).astype(BF16)
    misc = tails[0][8:16]
    for s in range(1, loaders):
        misc = misc + tails[s][8:16]
    probe_ref[...] = jnp.concatenate([misc[:, 0:cut], misc[:, 256 : 256 + cut]], axis=0).astype(BF16)
    gain_ref[...] = misc[0:1, 512 : 512 + cut].astype(BF16)
    loss_ref[...] = (misc[0:1, 768:769] + misc[1:2, 768:769] + misc[2:3, 768:769]) / texts
    d_caption = total_ref[...]
    for block_ref in refs[:blocks]:
        d_caption = d_caption + block_ref[...].astype(F32)
    unit = unit_ref[...]
    along = jnp.sum(d_caption * unit, axis=-1, keepdims=True)
    text_ref[...] = ((d_caption - unit * along) * inv_ref[:, 0:1]).astype(BF16)
    second.wait()


def local(
    patches, counts, owners, captions, norm_gain, key_probe, value_weight, logit_scale, logit_bias
):
    _, slots, rows, width = patches.shape
    heads = key_probe.shape[1]
    peers = lax.axis_size("fsdp")
    ranks = lax.axis_size("dp")
    cut = width // peers
    core = lax.axis_index("dp") % 2
    place = lax.axis_index("fsdp").astype(jnp.int32).reshape(1)
    scalars = jnp.concatenate([logit_scale, logit_bias])
    gain = norm_gain.reshape(1, width)
    probe = key_probe.T
    shape = jax.ShapeDtypeStruct
    dma = pltpu.SemaphoreType.DMA

    start = core * (cut - SEND_ROWS)
    part = lax.dynamic_slice_in_dim(value_weight, start, SEND_ROWS, axis=0)
    mine = lax.all_to_all(
        jnp.broadcast_to(part[None], (peers, SEND_ROWS, width)), "fsdp", 0, 0, tiled=True
    )

    lanes = slots * heads
    side, pooled = call(
        pool_body,
        [
            (shape((slots * rows, 2 * lanes), F32), vspec()),
            (shape((lanes, width), BF16), vspec()),
        ],
        [sspec(), sspec(), vspec(), vspec(), vspec()],
        40_000_000,
        4_000_000,
        [pltpu.VMEM((slots * rows, width), BF16)],
        name="pool",
    )(owners[0], counts[0], patches[0], gain, probe)

    caption_unit, caption_inv, texts = call(
        caption_body,
        [
            (shape((slots, width), F32), vspec()),
            (shape((slots, 128), F32), vspec()),
            (shape((slots, width), BF16), vspec()),
        ],
        [vspec()],
        40_000_000,
        4_000_000,
        name="caption",
    )(captions[0])
    if ranks > 2:
        for bit in (8, 4, 2):
            texts = jnp.concatenate([texts, swapped(texts, bit)], axis=0)
    mine, texts, pooled = lax.optimization_barrier((mine, texts, pooled))
    other = swapped(mine, 1)
    bits = [bit for bit in (SIDE_BIT, CORE_BIT, SIDE_BIT + CORE_BIT) if bit < ranks]
    flanks = [swapped(texts, bit) for bit in bits]
    full, sent = call(
        image_body,
        [
            (shape((STASH_ROWS, width), BF16), hspec()),
            (shape((peers, heads + slots, width), BF16), vspec()),
        ],
        [vspec()] * 5,
        400_000_000,
        6_000_000,
        [pltpu.VMEM((width + KEPT_ROWS, width), BF16), dma((2,))],
        name="image",
        limit=VMEM_IMAGE,
    )(mine, other, pooled, gain, probe)
    full, flanks = lax.optimization_barrier((full, flanks))
    got = lax.all_to_all(sent, "fsdp", 0, 0, tiled=True)
    texts = jnp.concatenate([texts] + flanks, axis=0)
    text_count = ranks * slots
    d_image_part, keep, send, loss_sums = call(
        pair_body,
        [
            (shape((peers, slots, width), BF16), vspec()),
            (shape((text_count // 2, width), F32), vspec()),
            (shape((text_count // 2, width), BF16), vspec()),
            (shape((slots, 128), F32), vspec()),
        ],
        [sspec(), sspec(), vspec(), vspec()],
        80_000_000,
        2_000_000,
        name="pair",
    )(place, scalars, got, texts)
    d_image_got = lax.all_to_all(d_image_part, "fsdp", 0, 0, tiled=True)

    def halves(rows_out):
        return [
            (shape((rows_out, width), F32), vspec()),
            (shape((rows_out, width), BF16), vspec()),
        ]

    def fold(keep, send, bit):
        if bit >= ranks:
            return keep, send
        return call(
            fold_body, halves(keep.shape[0] // 2), [vspec(), vspec()], 40_000_000, 1_000_000, name="fold"
        )(keep, swapped(send, bit))

    if ranks > 2:
        keep, send = fold(keep, send, CORE_BIT)
    if ranks > 2:
        keep, send = fold(keep, send, SIDE_BIT)

    outgoing = call(
        back_body,
        [(shape((peers, rows + 16, width), BF16), hspec())],
        [hspec()] * 6,
        500_000_000,
        8_000_000,
        [
            pltpu.SMEM((slots,), jnp.int32),
            pltpu.VMEM((peers, slots, width), BF16),
            pltpu.VMEM((width + KEPT_ROWS, width), BF16),
            pltpu.VMEM((slots, rows, width), BF16),
            pltpu.VMEM((slots * rows, 2 * lanes), F32),
            pltpu.VMEM((slots, 128), F32),
            pltpu.VMEM((slots * rows, width), F32),
            pltpu.VMEM((slots * rows, width), BF16),
            pltpu.VMEM((2 * lanes, width), BF16),
            pltpu.VMEM((peers, rows + 16, width), BF16),
            dma((12,)),
        ],
        name="back",
        limit=40_000_000,
    )(owners[0], d_image_got, full, patches, side, loss_sums)[0]
    outgoing, keep, send = lax.optimization_barrier((outgoing, keep, send))
    arrived = lax.all_to_all(outgoing, "fsdp", 0, 0, tiled=True)
    if ranks > 2:
        d_caption, *blocks = call(
            split_body,
            [(shape((slots, width), F32), vspec())] + [(shape((slots, width), BF16), vspec())] * 3,
            [vspec(), vspec()],
            40_000_000,
            1_000_000,
            name="split",
        )(keep, swapped(send, NEXT_BIT))
        blocks = [swapped(block, bit) for block, bit in zip(blocks, Z_BITS)]
    else:
        d_caption, blocks = keep, [swapped(send, CORE_BIT)]

    pooled_got = (
        got[:, :heads]
        .reshape(peers, heads, slots, cut)
        .transpose(1, 0, 2, 3)
        .reshape(heads, peers * slots, cut)
    )
    batch = ranks * peers * slots

    def last(*refs):
        last_body(*refs, blocks=len(blocks), texts=batch)

    row_grad, value_grad, probe_t, gain_grad, loss_part, text_grad = call(
        last,
        [
            (shape((1, slots, rows, width), BF16), hspec()),
            (shape((1, cut, width), BF16), vspec()),
            (shape((heads, cut), BF16), vspec()),
            (shape((1, cut), BF16), vspec()),
            (shape((1, 1), F32), vspec()),
            (shape((slots, width), BF16), vspec()),
        ],
        [hspec()] + [vspec()] * (4 + len(blocks)),
        400_000_000,
        3_000_000,
        [pltpu.VMEM((peers, 16, width), BF16), dma((2,))],
        name="last",
    )(arrived, pooled_got, d_caption, caption_unit, caption_inv, *blocks)

    return (loss_part, row_grad, text_grad[None], value_grad, probe_t.T[None], gain_grad)


def solution(mesh):
    placed = (
        P(("dp", "fsdp"), None, None, None),
        P(("dp", "fsdp"), None),
        P(("dp", "fsdp"), None),
        P(("dp", "fsdp"), None, None),
        P(),
        P(),
        P("fsdp", None),
        P(),
        P(),
    )
    return jax.shard_map(
        local,
        mesh=mesh,
        in_specs=placed,
        out_specs=(
            P("dp", "fsdp"),
            P(("dp", "fsdp"), None, None, None),
            P(("dp", "fsdp"), None, None),
            P("dp", "fsdp", None),
            P("dp", "fsdp", None),
            P("dp", "fsdp"),
        ),
        check_vma=False,
    )
```

```python
import math

import jax
import jax.numpy as jnp
from jax import lax
from jax.experimental import pallas as pl
from jax.experimental.pallas import tpu as pltpu
from jax.sharding import PartitionSpec as P

epsilon = 1e-06
F32 = jnp.float32
BF16 = jnp.bfloat16

VMEM_LIMIT = 16 * 1024 * 1024
VMEM_BACK = 40_000_000
VMEM_IMAGE = 28_000_000
KEPT_ROWS = 96
STASH_ROWS = 15_616
SEND_ROWS = 72


Z_BITS = (8, 4, 12)
NEXT_BIT, SIDE_BIT, CORE_BIT = 2, 16, 1


def swapped(block, bit):
    return lax.ppermute(block, "dp", [(i, i ^ bit) for i in range(lax.axis_size("dp"))])


def vspec():
    return pl.BlockSpec(memory_space=pltpu.VMEM)


def sspec():
    return pl.BlockSpec(memory_space=pltpu.SMEM)


def hspec():
    return pl.BlockSpec(memory_space=pltpu.HBM)


def call(body, outs, in_specs, flops, nbytes, scratch=(), name=None, limit=VMEM_LIMIT):
    return pl.pallas_call(
        body,
        out_shape=[shape for shape, _ in outs],
        in_specs=in_specs,
        out_specs=[spec for _, spec in outs],
        scratch_shapes=list(scratch),
        compiler_params=pltpu.CompilerParams(vmem_limit_bytes=limit),
        cost_estimate=pl.CostEstimate(flops=flops, bytes_accessed=nbytes, transcendentals=0),
        name=name,
    )


def source_of(owners, owner, slots):
    source = jnp.int32(0)
    for k in range(slots):
        source = source + jnp.where(owners[k] == owner, k, 0)
    return source


def nt_dot(a, b):
    return lax.dot_general(a, b, (((1,), (1,)), ((), ())), preferred_element_type=F32)


def tn_dot(a, b):
    return lax.dot_general(a, b, (((0,), (0,)), ((), ())), preferred_element_type=F32)


def terms(value):
    high = value.astype(BF16).astype(F32)
    middle = (value - high).astype(BF16).astype(F32)
    return [high, middle, value - high - middle]


def head_mask(heads, width):
    head_width = width // heads
    low = lax.broadcasted_iota(jnp.int32, (heads, width), 0) * head_width
    column = lax.broadcasted_iota(jnp.int32, (heads, width), 1)
    return ((column >= low) & (column < low + head_width)).astype(F32)


def pool_body(owners, counts, x_ref, gain_ref, probe_ref, side_ref, a_ref, scaled_ref):
    slots, rows, width = x_ref.shape
    heads = probe_ref.shape[0]
    scale = 1.0 / math.sqrt(width // heads)
    gain = gain_ref[...]
    lanes = slots * heads
    column = lax.broadcasted_iota(jnp.int32, (rows, lanes), 1)
    patch = lax.broadcasted_iota(jnp.int32, (rows, lanes), 0)
    masks = []
    for r in range(slots):
        source = source_of(owners, r, slots)
        x = x_ref[source].astype(F32)
        mean = jnp.sum(x, axis=-1, keepdims=True) * (1.0 / width)
        centered = x - mean
        var = jnp.sum(centered * centered, axis=-1, keepdims=True) * (1.0 / width)
        inv = lax.rsqrt(var + epsilon)
        scaled_ref[r * rows : (r + 1) * rows, :] = ((centered * inv) * gain).astype(BF16)
        side_ref[r * rows : (r + 1) * rows, 0:lanes] = jnp.where(column < lanes // 2, mean, inv)
        own = (column >= r * heads) & (column < (r + 1) * heads)
        masks.append(jnp.where(own & (patch < counts[source]), 1.0, 0.0))
    valid = jnp.concatenate(masks, axis=0) > 0.5
    scaled = scaled_ref[...]
    tiled = jnp.concatenate([probe_ref[...].astype(F32)] * slots, axis=0).astype(BF16)
    scores = nt_dot(scaled, tiled) * scale
    highest = jnp.max(jnp.where(valid, scores, -jnp.inf), axis=0, keepdims=True)
    raised = jnp.where(valid, jnp.exp(jnp.where(valid, scores - highest, 0.0)), 0.0)
    weights = raised / jnp.sum(raised, axis=0, keepdims=True)
    side_ref[:, lanes:] = weights
    a_ref[...] = tn_dot(weights.astype(BF16), scaled).astype(BF16)


def image_body(
    mine_ref, other_ref, a_ref, gain_ref, probe_ref, full_out, out_ref, full, sems
):
    shards, part_rows, width = mine_ref.shape
    slots = shards
    heads = a_ref.shape[0] // slots
    cut = width // shards
    rest = cut - part_rows
    core = lax.rem(lax.axis_index("dp"), 2)

    def put(low_ref, high_ref):
        for j in range(shards):
            full[j * cut : j * cut + part_rows, :] = low_ref[j]
            full[j * cut + part_rows : (j + 1) * cut, :] = high_ref[j, part_rows - rest :, :]

    @pl.when(core == 0)
    def _():
        put(mine_ref, other_ref)

    @pl.when(core != 0)
    def _():
        put(other_ref, mine_ref)

    copies = [
        pltpu.make_async_copy(full.at[at, :], full_out.at[at, :], sems.at[k])
        for k, at in enumerate([pl.ds(0, width), pl.ds(width, KEPT_ROWS)])
    ]
    copies[0].start()
    pooled = a_ref[...]
    wide = jnp.dot(pooled, full[0:width, :], preferred_element_type=F32).reshape(slots, heads, width)
    context = jnp.sum(wide * head_mask(heads, width)[None], axis=1)
    inv = lax.rsqrt(jnp.sum(context * context, axis=-1, keepdims=True) + epsilon)
    unit = context * inv
    kept = terms(unit) + terms(jnp.broadcast_to(inv, unit.shape))
    kept += terms(jnp.broadcast_to(gain_ref[...], unit.shape)) + [jnp.zeros_like(unit)]
    kept += [probe_ref[...].astype(F32)]
    full[width:, :] = jnp.concatenate(kept, axis=0).astype(BF16)
    copies[1].start()
    wide_pooled = pooled.astype(F32)
    for p in range(shards):
        moved = jnp.concatenate(
            [
                wide_pooled[b * heads : (b + 1) * heads, p * cut : (p + 1) * cut]
                for b in range(slots)
            ],
            axis=1,
        )
        out_ref[p] = jnp.concatenate([moved, unit], axis=0).astype(BF16)
    for copy in copies:
        copy.wait()


def caption_body(caption_ref, unit_ref, inv_ref, text_ref):
    caption = caption_ref[...].astype(F32)
    inv = lax.rsqrt(jnp.sum(caption * caption, axis=-1, keepdims=True) + epsilon)
    unit = caption * inv
    unit_ref[...] = unit
    inv_ref[...] = jnp.broadcast_to(inv, inv_ref.shape)
    text_ref[...] = unit.astype(BF16)


def pair_body(place, scalars, got_ref, text_ref, d_image_ref, loss_ref, keep_ref, *send_refs):
    loaders, got_rows, width = got_ref.shape
    slots = d_image_ref.shape[1]
    images = jnp.concatenate(
        [got_ref[s].astype(F32)[got_rows - slots :] for s in range(loaders)], axis=0
    ).astype(BF16)
    texts = text_ref[...]
    count = images.shape[0]
    text_count = texts.shape[0]
    scale = scalars[0]
    logits = scale * nt_dot(images, texts) + scalars[1]
    row = lax.broadcasted_iota(jnp.int32, (count, text_count), 0)
    column = lax.broadcasted_iota(jnp.int32, (count, text_count), 1)
    loader, owner = row // slots, row % slots
    matched = (owner == place[0]) & (column == loader)
    matched = matched.astype(F32)
    decay = jnp.exp(-jnp.abs(logits))
    signed = (1.0 - 2.0 * matched) * logits
    losses = jnp.maximum(signed, 0.0) + jnp.log1p(decay)
    sigmoid = jnp.where(logits >= 0.0, 1.0, decay) / (1.0 + decay)
    coefficient = (scale * (sigmoid - matched)).astype(BF16)
    d_image = jnp.dot(coefficient, texts, preferred_element_type=F32)
    d_image_ref[...] = d_image.reshape(d_image_ref.shape).astype(BF16)
    d_text = tn_dot(coefficient, images)
    part = keep_ref.shape[0]
    keep_ref[...] = d_text[:part]
    for k, send_ref in enumerate(send_refs):
        send_ref[...] = d_text[(k + 1) * part : (k + 2) * part].astype(BF16)
    per_image = jnp.sum(losses, axis=-1, keepdims=True)
    per_owner = jnp.sum(per_image.reshape(loaders, slots, 1), axis=0)
    loss_ref[...] = jnp.broadcast_to(per_owner, loss_ref.shape)


def fold_body(total_ref, *refs):
    *got_refs, keep_ref, send_ref = refs
    total = total_ref[...]
    for got_ref in got_refs:
        total = total + got_ref[...].astype(F32)
    half = keep_ref.shape[0]
    keep_ref[...] = total[:half]
    send_ref[...] = total[half:].astype(BF16)


def split_body(total_ref, got_ref, keep_ref, *block_refs):
    total = total_ref[...] + got_ref[...].astype(F32)
    rows = keep_ref.shape[0]
    keep_ref[...] = total[:rows]
    for k, block_ref in enumerate(block_refs):
        block_ref[...] = total[(k + 1) * rows : (k + 2) * rows].astype(BF16)


def finish_body(total_ref, unit_ref, inv_ref, *refs):
    d_caption = total_ref[...]
    for block_ref in refs[:-1]:
        d_caption = d_caption + block_ref[...].astype(F32)
    unit = unit_ref[...]
    along = jnp.sum(d_caption * unit, axis=-1, keepdims=True)
    refs[-1][...] = ((d_caption - unit * along) * inv_ref[:, 0:1]).astype(BF16)


def back_body(
    owners_in, got_ref, full_in, x_in, side_in, loss_in, out_ref,
    owners, full, x_ref, side_ref, loss_ref, normed_ref, scaled_ref, right, result, sems,
):
    slots, rows, width = x_ref.shape
    lanes = side_ref.shape[1] // 2
    heads = lanes // slots
    cut = width // slots
    scale = 1.0 / math.sqrt(width // heads)
    chunk = width // 3
    rows_of = [pl.ds(width, KEPT_ROWS)] + [pl.ds(c * chunk, chunk) for c in range(3)]
    pairs = [
        (full_in.at[rows_of[0], :], full.at[rows_of[0], :]),
        (owners_in, owners),
        (side_in, side_ref),
        (x_in.at[0], x_ref),
    ]
    pairs += [(full_in.at[at, :], full.at[at, :]) for at in rows_of[1:]]
    pairs += [(loss_in, loss_ref)]
    copies = [
        pltpu.make_async_copy(source, target, sems.at[k]) for k, (source, target) in enumerate(pairs)
    ]
    for copy in copies:
        copy.start()
    copies[0].wait()
    d_image = jnp.sum(got_ref[...].astype(F32), axis=0)
    kept = full[width:, :].astype(F32)

    def whole(first):
        return kept[first : first + 8] + kept[first + 8 : first + 16] + kept[first + 16 : first + 24]

    unit, inv_norm, gain = whole(0), whole(24), whole(48)[0:1]
    along = jnp.sum(d_image * unit, axis=-1, keepdims=True)
    d_context = (d_image - unit * along) * inv_norm
    d_context = d_context.astype(BF16).astype(F32)
    right[lanes:, :] = jnp.concatenate([kept[80 : 80 + heads]] * slots, axis=0).astype(BF16)
    spread = (d_context[:, None, :] * head_mask(heads, width)[None]).reshape(lanes, width).astype(BF16)
    for copy in copies[1:4]:
        copy.wait()
    for r in range(slots):
        at = slice(r * rows, (r + 1) * rows)
        x = x_ref[source_of(owners, r, slots)].astype(F32)
        normed = (x - side_ref[at, 0:1]) * side_ref[at, lanes // 2 : lanes // 2 + 1]
        normed_ref[at, :] = normed
        scaled_ref[at, :] = (normed * gain).astype(BF16)
    for c in range(3):
        copies[4 + c].wait()
        at = slice(c * chunk, (c + 1) * chunk)
        right[0:lanes, at] = nt_dot(spread, full[at, :]).astype(BF16)
    scaled = scaled_ref[...]
    weights = side_ref[:, lanes:]
    d_weights = nt_dot(scaled, right[0:lanes, :])
    centre = jnp.sum(weights * d_weights, axis=0, keepdims=True)
    d_scores = (weights * (d_weights - centre) * scale).astype(BF16)
    left = jnp.concatenate([weights.astype(BF16), d_scores], axis=1)
    gain_total = jnp.zeros((8, width), F32)
    sent = []
    half = slots // 2
    for g in range(2):
        d_scaled_half = jnp.dot(
            left[g * half * rows : (g + 1) * half * rows], right[...], preferred_element_type=F32
        )
        for k in range(half):
            r = g * half + k
            at = slice(r * rows, (r + 1) * rows)
            d_scaled = d_scaled_half[k * rows : (k + 1) * rows]
            normed = normed_ref[at, :]
            product = d_scaled * normed
            gain_total = gain_total + jnp.sum(product.reshape(rows // 8, 8, width), axis=0)
            grad_in = d_scaled * gain
            mean_a = jnp.sum(grad_in, axis=-1, keepdims=True) * (1.0 / width)
            mean_b = jnp.sum(product * gain, axis=-1, keepdims=True) * (1.0 / width)
            inv = side_ref[at, lanes // 2 : lanes // 2 + 1]
            result[r, 0:rows, :] = (inv * (grad_in - mean_a - normed * mean_b)).astype(BF16)
        at = pl.ds(g * half, half)
        copy = pltpu.make_async_copy(
            result.at[at, pl.ds(0, rows), :], out_ref.at[at, pl.ds(0, rows), :], sems.at[9 + g]
        )
        copy.start()
        sent.append(copy)
    probe_total = jnp.sum(tn_dot(d_scores, scaled).reshape(slots, heads, width), axis=0)
    gain_sum = jnp.sum(gain_total, axis=0, keepdims=True)
    copies[7].wait()
    high, middle, low = terms(loss_ref[...])
    pad = jnp.zeros((8, 256 - cut), F32)
    for p in range(slots):
        at = slice(p * cut, (p + 1) * cut)
        losses = jnp.concatenate(
            [high[p : p + 1], middle[p : p + 1], low[p : p + 1], jnp.zeros((5, 128), F32)], axis=0
        )
        misc = jnp.concatenate(
            [
                probe_total[0:8, at],
                pad,
                probe_total[8:16, at],
                pad,
                jnp.broadcast_to(gain_sum[:, at], (8, cut)),
                pad,
                losses,
                jnp.zeros((8, width - 896), F32),
            ],
            axis=1,
        )
        result[p, rows : rows + 16, :] = jnp.concatenate([d_context, misc], axis=0).astype(BF16)
    tail = pl.ds(rows, 16)
    copy = pltpu.make_async_copy(
        result.at[:, tail, :], out_ref.at[:, tail, :], sems.at[11]
    )
    copy.start()
    for copy in sent + [copy]:
        copy.wait()


def last_body(got_ref, a_ref, row_ref, value_ref, probe_ref, gain_ref, loss_ref, tail, sems, *, texts):
    loaders, got_rows, width = got_ref.shape
    rows = row_ref.shape[2]
    heads, images, cut = a_ref.shape
    head_width = width // heads
    first = pltpu.make_async_copy(got_ref.at[:, pl.ds(rows, 16), :], tail, sems.at[0])
    first.start()
    second = pltpu.make_async_copy(got_ref.at[:, pl.ds(0, rows), :], row_ref.at[0], sems.at[1])
    second.start()
    first.wait()
    tails = [tail[s].astype(F32) for s in range(loaders)]
    d_context = jnp.concatenate([t[0:8] for t in tails], axis=0)
    mask = head_mask(heads, width)
    tiles = [None] * (width // 128)
    for h in range(heads):
        low, high = h * head_width // 128, -(-(h + 1) * head_width // 128)
        lanes = slice(low * 128, high * 128)
        part = tn_dot(a_ref[h], (d_context[:, lanes] * mask[h : h + 1, lanes]).astype(BF16))
        for t in range(low, high):
            piece = part[:, (t - low) * 128 : (t - low + 1) * 128]
            tiles[t] = piece if tiles[t] is None else tiles[t] + piece
    value_ref[0] = jnp.concatenate(tiles, axis=1).astype(BF16)
    misc = tails[0][8:16]
    for s in range(1, loaders):
        misc = misc + tails[s][8:16]
    probe_ref[...] = jnp.concatenate([misc[:, 0:cut], misc[:, 256 : 256 + cut]], axis=0).astype(BF16)
    gain_ref[...] = misc[0:1, 512 : 512 + cut].astype(BF16)
    loss_ref[...] = (misc[0:1, 768:769] + misc[1:2, 768:769] + misc[2:3, 768:769]) / texts
    second.wait()


def local(
    patches, counts, owners, captions, norm_gain, key_probe, value_weight, logit_scale, logit_bias
):
    _, slots, rows, width = patches.shape
    heads = key_probe.shape[1]
    peers = lax.axis_size("fsdp")
    ranks = lax.axis_size("dp")
    cut = width // peers
    core = lax.axis_index("dp") % 2
    place = lax.axis_index("fsdp").astype(jnp.int32).reshape(1)
    scalars = jnp.concatenate([logit_scale, logit_bias])
    gain = norm_gain.reshape(1, width)
    probe = key_probe.T
    shape = jax.ShapeDtypeStruct
    dma = pltpu.SemaphoreType.DMA

    start = core * (cut - SEND_ROWS)
    part = lax.dynamic_slice_in_dim(value_weight, start, SEND_ROWS, axis=0)
    mine = lax.all_to_all(
        jnp.broadcast_to(part[None], (peers, SEND_ROWS, width)), "fsdp", 0, 0, tiled=True
    )

    lanes = slots * heads
    side, pooled = call(
        pool_body,
        [
            (shape((slots * rows, 2 * lanes), F32), vspec()),
            (shape((lanes, width), BF16), vspec()),
        ],
        [sspec(), sspec(), vspec(), vspec(), vspec()],
        40_000_000,
        4_000_000,
        [pltpu.VMEM((slots * rows, width), BF16)],
        name="pool",
    )(owners[0], counts[0], patches[0], gain, probe)

    caption_unit, caption_inv, texts = call(
        caption_body,
        [
            (shape((slots, width), F32), vspec()),
            (shape((slots, 128), F32), vspec()),
            (shape((slots, width), BF16), vspec()),
        ],
        [vspec()],
        40_000_000,
        4_000_000,
        name="caption",
    )(captions[0])
    if ranks > 2:
        for bit in (8, 4, 2):
            texts = jnp.concatenate([texts, swapped(texts, bit)], axis=0)
    mine, texts, pooled = lax.optimization_barrier((mine, texts, pooled))
    other = swapped(mine, 1)
    bits = [bit for bit in (SIDE_BIT, CORE_BIT, SIDE_BIT + CORE_BIT) if bit < ranks]
    flanks = [swapped(texts, bit) for bit in bits]
    full, sent = call(
        image_body,
        [
            (shape((STASH_ROWS, width), BF16), hspec()),
            (shape((peers, heads + slots, width), BF16), vspec()),
        ],
        [vspec()] * 5,
        400_000_000,
        6_000_000,
        [pltpu.VMEM((width + KEPT_ROWS, width), BF16), dma((2,))],
        name="image",
        limit=VMEM_IMAGE,
    )(mine, other, pooled, gain, probe)
    full, flanks = lax.optimization_barrier((full, flanks))
    got = lax.all_to_all(sent, "fsdp", 0, 0, tiled=True)
    texts = jnp.concatenate([texts] + flanks, axis=0)
    text_count = ranks * slots
    parts_of = len(bits) + 1
    d_image_part, loss_sums, keep, *sends = call(
        pair_body,
        [
            (shape((peers, slots, width), BF16), vspec()),
            (shape((slots, 128), F32), vspec()),
            (shape((text_count // parts_of, width), F32), vspec()),
        ]
        + [(shape((text_count // parts_of, width), BF16), vspec())] * len(bits),
        [sspec(), sspec(), vspec(), vspec()],
        80_000_000,
        2_000_000,
        name="pair",
    )(place, scalars, got, texts)
    d_image_got = lax.all_to_all(d_image_part, "fsdp", 0, 0, tiled=True)

    def halves(rows_out):
        return [
            (shape((rows_out, width), F32), vspec()),
            (shape((rows_out, width), BF16), vspec()),
        ]

    send = sends[0]
    if ranks > 2:
        keep, send = call(
            fold_body,
            halves(keep.shape[0] // 2),
            [vspec()] * (1 + len(bits)),
            40_000_000,
            1_000_000,
            name="fold",
        )(keep, *[swapped(block, bit) for block, bit in zip(sends, bits)])

    outgoing = call(
        back_body,
        [(shape((peers, rows + 16, width), BF16), hspec())],
        [hspec(), vspec()] + [hspec()] * 4,
        500_000_000,
        8_000_000,
        [
            pltpu.SMEM((slots,), jnp.int32),
            pltpu.VMEM((width + KEPT_ROWS, width), BF16),
            pltpu.VMEM((slots, rows, width), BF16),
            pltpu.VMEM((slots * rows, 2 * lanes), F32),
            pltpu.VMEM((slots, 128), F32),
            pltpu.VMEM((slots * rows, width), F32),
            pltpu.VMEM((slots * rows, width), BF16),
            pltpu.VMEM((2 * lanes, width), BF16),
            pltpu.VMEM((peers, rows + 16, width), BF16),
            dma((12,)),
        ],
        name="back",
        limit=VMEM_BACK,
    )(owners[0], d_image_got, full, patches, side, loss_sums)[0]
    outgoing, keep, send = lax.optimization_barrier((outgoing, keep, send))
    arrived = lax.all_to_all(outgoing, "fsdp", 0, 0, tiled=True)
    if ranks > 2:
        d_caption, *blocks = call(
            split_body,
            [(shape((slots, width), F32), vspec())] + [(shape((slots, width), BF16), vspec())] * 3,
            [vspec(), vspec()],
            40_000_000,
            1_000_000,
            name="split",
        )(keep, swapped(send, NEXT_BIT))
        blocks = [swapped(block, bit) for block, bit in zip(blocks, Z_BITS)]
    else:
        d_caption, blocks = keep, [swapped(send, CORE_BIT)]

    pooled_got = (
        got[:, :heads]
        .reshape(peers, heads, slots, cut)
        .transpose(1, 0, 2, 3)
        .reshape(heads, peers * slots, cut)
    )
    batch = ranks * peers * slots

    def last(*refs):
        last_body(*refs, texts=batch)

    row_grad, value_grad, probe_t, gain_grad, loss_part = call(
        last,
        [
            (shape((1, slots, rows, width), BF16), hspec()),
            (shape((1, cut, width), BF16), vspec()),
            (shape((heads, cut), BF16), vspec()),
            (shape((1, cut), BF16), vspec()),
            (shape((1, 1), F32), vspec()),
        ],
        [hspec(), vspec()],
        400_000_000,
        3_000_000,
        [pltpu.VMEM((peers, 16, width), BF16), dma((2,))],
        name="last",
    )(arrived, pooled_got)

    loss_part, blocks = lax.optimization_barrier((loss_part, blocks))
    text_grad = call(
        finish_body,
        [(shape((slots, width), BF16), vspec())],
        [vspec()] * (3 + len(blocks)),
        0,
        0,
        name="finish",
    )(d_caption, caption_unit, caption_inv, *blocks)[0]

    return (loss_part, row_grad, text_grad[None], value_grad, probe_t.T[None], gain_grad)


def solution(mesh):
    placed = (
        P(("dp", "fsdp"), None, None, None),
        P(("dp", "fsdp"), None),
        P(("dp", "fsdp"), None),
        P(("dp", "fsdp"), None, None),
        P(),
        P(),
        P("fsdp", None),
        P(),
        P(),
    )
    return jax.shard_map(
        local,
        mesh=mesh,
        in_specs=placed,
        out_specs=(
            P("dp", "fsdp"),
            P(("dp", "fsdp"), None, None, None),
            P(("dp", "fsdp"), None, None),
            P("dp", "fsdp", None),
            P("dp", "fsdp", None),
            P("dp", "fsdp"),
        ),
        check_vma=False,
    )
```

```python
import math

import jax
import jax.numpy as jnp
from jax import lax
from jax.experimental import pallas as pl
from jax.experimental.pallas import tpu as pltpu
from jax.sharding import PartitionSpec as P

epsilon = 1e-06
F32 = jnp.float32
BF16 = jnp.bfloat16

VMEM_LIMIT = 16 * 1024 * 1024
VMEM_BACK = 40_000_000
VMEM_IMAGE = 28_000_000
KEPT_ROWS = 96
STASH_ROWS = 15_616
SEND_ROWS = 72


Z_BITS = (8, 4, 12)
NEXT_BIT, SIDE_BIT, CORE_BIT = 2, 16, 1


def swapped(block, bit):
    return lax.ppermute(block, "dp", [(i, i ^ bit) for i in range(lax.axis_size("dp"))])


def vspec():
    return pl.BlockSpec(memory_space=pltpu.VMEM)


def sspec():
    return pl.BlockSpec(memory_space=pltpu.SMEM)


def hspec():
    return pl.BlockSpec(memory_space=pltpu.HBM)


def call(body, outs, in_specs, flops, nbytes, scratch=(), name=None, limit=VMEM_LIMIT):
    return pl.pallas_call(
        body,
        out_shape=[shape for shape, _ in outs],
        in_specs=in_specs,
        out_specs=[spec for _, spec in outs],
        scratch_shapes=list(scratch),
        compiler_params=pltpu.CompilerParams(vmem_limit_bytes=limit),
        cost_estimate=pl.CostEstimate(flops=flops, bytes_accessed=nbytes, transcendentals=0),
        name=name,
    )


def source_of(owners, owner, slots):
    source = jnp.int32(0)
    for k in range(slots):
        source = source + jnp.where(owners[k] == owner, k, 0)
    return source


def nt_dot(a, b):
    return lax.dot_general(a, b, (((1,), (1,)), ((), ())), preferred_element_type=F32)


def tn_dot(a, b):
    return lax.dot_general(a, b, (((0,), (0,)), ((), ())), preferred_element_type=F32)


def terms(value):
    high = value.astype(BF16).astype(F32)
    middle = (value - high).astype(BF16).astype(F32)
    return [high, middle, value - high - middle]


def head_mask(heads, width):
    head_width = width // heads
    low = lax.broadcasted_iota(jnp.int32, (heads, width), 0) * head_width
    column = lax.broadcasted_iota(jnp.int32, (heads, width), 1)
    return ((column >= low) & (column < low + head_width)).astype(F32)


def pool_body(owners, counts, x_ref, gain_ref, probe_ref, side_ref, a_ref, scaled_ref):
    slots, rows, width = x_ref.shape
    heads = probe_ref.shape[0]
    scale = 1.0 / math.sqrt(width // heads)
    gain = gain_ref[...]
    lanes = slots * heads
    column = lax.broadcasted_iota(jnp.int32, (rows, lanes), 1)
    patch = lax.broadcasted_iota(jnp.int32, (rows, lanes), 0)
    masks = []
    for r in range(slots):
        source = source_of(owners, r, slots)
        x = x_ref[source].astype(F32)
        mean = jnp.sum(x, axis=-1, keepdims=True) * (1.0 / width)
        centered = x - mean
        var = jnp.sum(centered * centered, axis=-1, keepdims=True) * (1.0 / width)
        inv = lax.rsqrt(var + epsilon)
        scaled_ref[r * rows : (r + 1) * rows, :] = ((centered * inv) * gain).astype(BF16)
        side_ref[r * rows : (r + 1) * rows, 0:lanes] = jnp.where(column < lanes // 2, mean, inv)
        own = (column >= r * heads) & (column < (r + 1) * heads)
        masks.append(jnp.where(own & (patch < counts[source]), 1.0, 0.0))
    valid = jnp.concatenate(masks, axis=0) > 0.5
    scaled = scaled_ref[...]
    tiled = jnp.concatenate([probe_ref[...].astype(F32)] * slots, axis=0).astype(BF16)
    scores = nt_dot(scaled, tiled) * scale
    highest = jnp.max(jnp.where(valid, scores, -jnp.inf), axis=0, keepdims=True)
    raised = jnp.where(valid, jnp.exp(jnp.where(valid, scores - highest, 0.0)), 0.0)
    weights = raised / jnp.sum(raised, axis=0, keepdims=True)
    side_ref[:, lanes:] = weights
    a_ref[...] = tn_dot(weights.astype(BF16), scaled).astype(BF16)


def image_body(
    mine_ref, other_ref, a_ref, gain_ref, probe_ref, full_out, out_ref, full, sems
):
    shards, part_rows, width = mine_ref.shape
    slots = shards
    heads = a_ref.shape[0] // slots
    cut = width // shards
    rest = cut - part_rows
    core = lax.rem(lax.axis_index("dp"), 2)

    def put(low_ref, high_ref):
        for j in range(shards):
            full[j * cut : j * cut + part_rows, :] = low_ref[j]
            full[j * cut + part_rows : (j + 1) * cut, :] = high_ref[j, part_rows - rest :, :]

    @pl.when(core == 0)
    def _():
        put(mine_ref, other_ref)

    @pl.when(core != 0)
    def _():
        put(other_ref, mine_ref)

    copies = [
        pltpu.make_async_copy(full.at[at, :], full_out.at[at, :], sems.at[k])
        for k, at in enumerate([pl.ds(0, width), pl.ds(width, KEPT_ROWS)])
    ]
    copies[0].start()
    pooled = a_ref[...]
    wide = jnp.dot(pooled, full[0:width, :], preferred_element_type=F32).reshape(slots, heads, width)
    context = jnp.sum(wide * head_mask(heads, width)[None], axis=1)
    inv = lax.rsqrt(jnp.sum(context * context, axis=-1, keepdims=True) + epsilon)
    unit = context * inv
    kept = terms(unit) + terms(jnp.broadcast_to(inv, unit.shape))
    kept += terms(jnp.broadcast_to(gain_ref[...], unit.shape)) + [jnp.zeros_like(unit)]
    kept += [probe_ref[...].astype(F32)]
    full[width:, :] = jnp.concatenate(kept, axis=0).astype(BF16)
    copies[1].start()
    wide_pooled = pooled.astype(F32)
    for p in range(shards):
        moved = jnp.concatenate(
            [
                wide_pooled[b * heads : (b + 1) * heads, p * cut : (p + 1) * cut]
                for b in range(slots)
            ],
            axis=1,
        )
        out_ref[p] = jnp.concatenate([moved, unit], axis=0).astype(BF16)
    for copy in copies:
        copy.wait()


def caption_body(caption_ref, unit_ref, inv_ref, text_ref):
    caption = caption_ref[...].astype(F32)
    inv = lax.rsqrt(jnp.sum(caption * caption, axis=-1, keepdims=True) + epsilon)
    unit = caption * inv
    unit_ref[...] = unit
    inv_ref[...] = jnp.broadcast_to(inv, inv_ref.shape)
    text_ref[...] = unit.astype(BF16)


def pair_body(scalars, got_ref, text_ref, d_image_ref, loss_ref, keep_ref, *send_refs):
    loaders, got_rows, width = got_ref.shape
    slots = d_image_ref.shape[1]
    images = jnp.concatenate(
        [got_ref[s].astype(F32)[got_rows - slots :] for s in range(loaders)], axis=0
    ).astype(BF16)
    texts = text_ref[...]
    count = images.shape[0]
    text_count = texts.shape[0]
    scale = scalars[0:1, 0:1]
    logits = scale * nt_dot(images, texts) + scalars[1:2, 0:1]
    row = lax.broadcasted_iota(jnp.int32, (count, text_count), 0)
    column = lax.broadcasted_iota(jnp.int32, (count, text_count), 1)
    loader, owner = row // slots, row % slots
    matched = (owner == lax.axis_index("fsdp")) & (column == loader)
    matched = matched.astype(F32)
    decay = jnp.exp(-jnp.abs(logits))
    signed = (1.0 - 2.0 * matched) * logits
    losses = jnp.maximum(signed, 0.0) + jnp.log1p(decay)
    sigmoid = jnp.where(logits >= 0.0, 1.0, decay) / (1.0 + decay)
    coefficient = (scale * (sigmoid - matched)).astype(BF16)
    d_image = jnp.dot(coefficient, texts, preferred_element_type=F32)
    d_image_ref[...] = d_image.reshape(d_image_ref.shape).astype(BF16)
    d_text = tn_dot(coefficient, images)
    part = keep_ref.shape[0]
    keep_ref[...] = d_text[:part]
    for k, send_ref in enumerate(send_refs):
        send_ref[...] = d_text[(k + 1) * part : (k + 2) * part].astype(BF16)
    per_image = jnp.sum(losses, axis=-1, keepdims=True)
    per_owner = jnp.sum(per_image.reshape(loaders, slots, 1), axis=0)
    loss_ref[...] = jnp.broadcast_to(per_owner, loss_ref.shape)


def fold_body(total_ref, *refs):
    *got_refs, keep_ref, send_ref = refs
    total = total_ref[...]
    for got_ref in got_refs:
        total = total + got_ref[...].astype(F32)
    half = keep_ref.shape[0]
    keep_ref[...] = total[:half]
    send_ref[...] = total[half:].astype(BF16)


def split_body(total_ref, got_ref, keep_ref, *block_refs):
    total = total_ref[...] + got_ref[...].astype(F32)
    rows = keep_ref.shape[0]
    keep_ref[...] = total[:rows]
    for k, block_ref in enumerate(block_refs):
        block_ref[...] = total[(k + 1) * rows : (k + 2) * rows].astype(BF16)


def finish_body(total_ref, unit_ref, inv_ref, *refs):
    d_caption = total_ref[...]
    for block_ref in refs[:-1]:
        d_caption = d_caption + block_ref[...].astype(F32)
    unit = unit_ref[...]
    along = jnp.sum(d_caption * unit, axis=-1, keepdims=True)
    refs[-1][...] = ((d_caption - unit * along) * inv_ref[:, 0:1]).astype(BF16)


def back_body(
    owners_in, got_ref, full_in, x_in, side_in, loss_in, out_ref,
    owners, full, x_ref, side_ref, loss_ref, normed_ref, scaled_ref, right, result, sems,
):
    slots, rows, width = x_ref.shape
    lanes = side_ref.shape[1] // 2
    heads = lanes // slots
    cut = width // slots
    scale = 1.0 / math.sqrt(width // heads)
    chunk = width // 3
    rows_of = [pl.ds(width, KEPT_ROWS)] + [pl.ds(c * chunk, chunk) for c in range(3)]
    pairs = [
        (full_in.at[rows_of[0], :], full.at[rows_of[0], :]),
        (owners_in, owners),
        (side_in, side_ref),
        (x_in.at[0], x_ref),
    ]
    pairs += [(full_in.at[at, :], full.at[at, :]) for at in rows_of[1:]]
    pairs += [(loss_in, loss_ref)]
    copies = [
        pltpu.make_async_copy(source, target, sems.at[k]) for k, (source, target) in enumerate(pairs)
    ]
    for copy in copies:
        copy.start()
    copies[0].wait()
    d_image = jnp.sum(got_ref[...].astype(F32), axis=0)
    kept = full[width:, :].astype(F32)

    def whole(first):
        return kept[first : first + 8] + kept[first + 8 : first + 16] + kept[first + 16 : first + 24]

    unit, inv_norm, gain = whole(0), whole(24), whole(48)[0:1]
    along = jnp.sum(d_image * unit, axis=-1, keepdims=True)
    d_context = (d_image - unit * along) * inv_norm
    d_context = d_context.astype(BF16).astype(F32)
    right[lanes:, :] = jnp.concatenate([kept[80 : 80 + heads]] * slots, axis=0).astype(BF16)
    spread = (d_context[:, None, :] * head_mask(heads, width)[None]).reshape(lanes, width).astype(BF16)
    for copy in copies[1:4]:
        copy.wait()
    for r in range(slots):
        at = slice(r * rows, (r + 1) * rows)
        x = x_ref[source_of(owners, r, slots)].astype(F32)
        normed = (x - side_ref[at, 0:1]) * side_ref[at, lanes // 2 : lanes // 2 + 1]
        normed_ref[at, :] = normed
        scaled_ref[at, :] = (normed * gain).astype(BF16)
    for c in range(3):
        copies[4 + c].wait()
        at = slice(c * chunk, (c + 1) * chunk)
        right[0:lanes, at] = nt_dot(spread, full[at, :]).astype(BF16)
    scaled = scaled_ref[...]
    weights = side_ref[:, lanes:]
    d_weights = nt_dot(scaled, right[0:lanes, :])
    centre = jnp.sum(weights * d_weights, axis=0, keepdims=True)
    d_scores = (weights * (d_weights - centre) * scale).astype(BF16)
    left = jnp.concatenate([weights.astype(BF16), d_scores], axis=1)
    gain_total = jnp.zeros((8, width), F32)
    sent = []
    half = slots // 2
    for g in range(2):
        d_scaled_half = jnp.dot(
            left[g * half * rows : (g + 1) * half * rows], right[...], preferred_element_type=F32
        )
        for k in range(half):
            r = g * half + k
            at = slice(r * rows, (r + 1) * rows)
            d_scaled = d_scaled_half[k * rows : (k + 1) * rows]
            normed = normed_ref[at, :]
            product = d_scaled * normed
            gain_total = gain_total + jnp.sum(product.reshape(rows // 8, 8, width), axis=0)
            grad_in = d_scaled * gain
            mean_a = jnp.sum(grad_in, axis=-1, keepdims=True) * (1.0 / width)
            mean_b = jnp.sum(product * gain, axis=-1, keepdims=True) * (1.0 / width)
            inv = side_ref[at, lanes // 2 : lanes // 2 + 1]
            result[r, 0:rows, :] = (inv * (grad_in - mean_a - normed * mean_b)).astype(BF16)
        at = pl.ds(g * half, half)
        copy = pltpu.make_async_copy(
            result.at[at, pl.ds(0, rows), :], out_ref.at[at, pl.ds(0, rows), :], sems.at[9 + g]
        )
        copy.start()
        sent.append(copy)
    probe_total = jnp.sum(tn_dot(d_scores, scaled).reshape(slots, heads, width), axis=0)
    gain_sum = jnp.sum(gain_total, axis=0, keepdims=True)
    copies[7].wait()
    high, middle, low = terms(loss_ref[...])
    pad = jnp.zeros((8, 256 - cut), F32)
    for p in range(slots):
        at = slice(p * cut, (p + 1) * cut)
        losses = jnp.concatenate(
            [high[p : p + 1], middle[p : p + 1], low[p : p + 1], jnp.zeros((5, 128), F32)], axis=0
        )
        misc = jnp.concatenate(
            [
                probe_total[0:8, at],
                pad,
                probe_total[8:16, at],
                pad,
                jnp.broadcast_to(gain_sum[:, at], (8, cut)),
                pad,
                losses,
                jnp.zeros((8, width - 896), F32),
            ],
            axis=1,
        )
        result[p, rows : rows + 16, :] = jnp.concatenate([d_context, misc], axis=0).astype(BF16)
    tail = pl.ds(rows, 16)
    copy = pltpu.make_async_copy(
        result.at[:, tail, :], out_ref.at[:, tail, :], sems.at[11]
    )
    copy.start()
    for copy in sent + [copy]:
        copy.wait()


def last_body(got_ref, a_ref, row_ref, value_ref, probe_ref, gain_ref, loss_ref, tail, sems, *, texts):
    loaders, got_rows, width = got_ref.shape
    rows = row_ref.shape[2]
    heads, images, cut = a_ref.shape
    head_width = width // heads
    first = pltpu.make_async_copy(got_ref.at[:, pl.ds(rows, 16), :], tail, sems.at[0])
    first.start()
    second = pltpu.make_async_copy(got_ref.at[:, pl.ds(0, rows), :], row_ref.at[0], sems.at[1])
    second.start()
    first.wait()
    tails = [tail[s].astype(F32) for s in range(loaders)]
    d_context = jnp.concatenate([t[0:8] for t in tails], axis=0)
    mask = head_mask(heads, width)
    tiles = [None] * (width // 128)
    for h in range(heads):
        low, high = h * head_width // 128, -(-(h + 1) * head_width // 128)
        lanes = slice(low * 128, high * 128)
        part = tn_dot(a_ref[h], (d_context[:, lanes] * mask[h : h + 1, lanes]).astype(BF16))
        for t in range(low, high):
            piece = part[:, (t - low) * 128 : (t - low + 1) * 128]
            tiles[t] = piece if tiles[t] is None else tiles[t] + piece
    value_ref[0] = jnp.concatenate(tiles, axis=1).astype(BF16)
    misc = tails[0][8:16]
    for s in range(1, loaders):
        misc = misc + tails[s][8:16]
    probe_ref[...] = jnp.concatenate([misc[:, 0:cut], misc[:, 256 : 256 + cut]], axis=0).astype(BF16)
    gain_ref[...] = misc[0:1, 512 : 512 + cut].astype(BF16)
    loss_ref[...] = (misc[0:1, 768:769] + misc[1:2, 768:769] + misc[2:3, 768:769]) / texts
    second.wait()


def local(
    patches, counts, owners, captions, norm_gain, key_probe, value_weight, logit_scale, logit_bias
):
    _, slots, rows, width = patches.shape
    heads = key_probe.shape[1]
    peers = lax.axis_size("fsdp")
    ranks = lax.axis_size("dp")
    cut = width // peers
    core = lax.axis_index("dp") % 2
    scalars = jnp.broadcast_to(jnp.stack([logit_scale, logit_bias]), (2, 128))
    gain = norm_gain.reshape(1, width)
    probe = key_probe.T
    shape = jax.ShapeDtypeStruct
    dma = pltpu.SemaphoreType.DMA

    start = core * (cut - SEND_ROWS)
    part = lax.dynamic_slice_in_dim(value_weight, start, SEND_ROWS, axis=0)
    mine = lax.all_to_all(
        jnp.broadcast_to(part[None], (peers, SEND_ROWS, width)), "fsdp", 0, 0, tiled=True
    )

    lanes = slots * heads
    side, pooled = call(
        pool_body,
        [
            (shape((slots * rows, 2 * lanes), F32), vspec()),
            (shape((lanes, width), BF16), vspec()),
        ],
        [sspec(), sspec(), vspec(), vspec(), vspec()],
        40_000_000,
        4_000_000,
        [pltpu.VMEM((slots * rows, width), BF16)],
        name="pool",
    )(owners[0], counts[0], patches[0], gain, probe)

    caption_unit, caption_inv, texts = call(
        caption_body,
        [
            (shape((slots, width), F32), vspec()),
            (shape((slots, 128), F32), vspec()),
            (shape((slots, width), BF16), vspec()),
        ],
        [vspec()],
        40_000_000,
        4_000_000,
        name="caption",
    )(captions[0])
    if ranks > 2:
        for bit in (8, 4, 2):
            texts = jnp.concatenate([texts, swapped(texts, bit)], axis=0)
    mine, texts, pooled = lax.optimization_barrier((mine, texts, pooled))
    other = swapped(mine, 1)
    bits = [bit for bit in (SIDE_BIT, CORE_BIT, SIDE_BIT + CORE_BIT) if bit < ranks]
    flanks = [swapped(texts, bit) for bit in bits]
    full, sent = call(
        image_body,
        [
            (shape((STASH_ROWS, width), BF16), hspec()),
            (shape((peers, heads + slots, width), BF16), vspec()),
        ],
        [vspec()] * 5,
        400_000_000,
        6_000_000,
        [pltpu.VMEM((width + KEPT_ROWS, width), BF16), dma((2,))],
        name="image",
        limit=VMEM_IMAGE,
    )(mine, other, pooled, gain, probe)
    full, flanks = lax.optimization_barrier((full, flanks))
    got = lax.all_to_all(sent, "fsdp", 0, 0, tiled=True)
    texts = jnp.concatenate([texts] + flanks, axis=0)
    text_count = ranks * slots
    parts_of = len(bits) + 1
    d_image_part, loss_sums, keep, *sends = call(
        pair_body,
        [
            (shape((peers, slots, width), BF16), vspec()),
            (shape((slots, 128), F32), vspec()),
            (shape((text_count // parts_of, width), F32), vspec()),
        ]
        + [(shape((text_count // parts_of, width), BF16), vspec())] * len(bits),
        [vspec(), vspec(), vspec()],
        80_000_000,
        2_000_000,
        name="pair",
    )(scalars, got, texts)
    d_image_got = lax.all_to_all(d_image_part, "fsdp", 0, 0, tiled=True)

    def halves(rows_out):
        return [
            (shape((rows_out, width), F32), vspec()),
            (shape((rows_out, width), BF16), vspec()),
        ]

    send = sends[0]
    if ranks > 2:
        keep, send = call(
            fold_body,
            halves(keep.shape[0] // 2),
            [vspec()] * (1 + len(bits)),
            40_000_000,
            1_000_000,
            name="fold",
        )(keep, *[swapped(block, bit) for block, bit in zip(sends, bits)])

    outgoing = call(
        back_body,
        [(shape((peers, rows + 16, width), BF16), hspec())],
        [hspec(), vspec()] + [hspec()] * 4,
        500_000_000,
        8_000_000,
        [
            pltpu.SMEM((slots,), jnp.int32),
            pltpu.VMEM((width + KEPT_ROWS, width), BF16),
            pltpu.VMEM((slots, rows, width), BF16),
            pltpu.VMEM((slots * rows, 2 * lanes), F32),
            pltpu.VMEM((slots, 128), F32),
            pltpu.VMEM((slots * rows, width), F32),
            pltpu.VMEM((slots * rows, width), BF16),
            pltpu.VMEM((2 * lanes, width), BF16),
            pltpu.VMEM((peers, rows + 16, width), BF16),
            dma((12,)),
        ],
        name="back",
        limit=VMEM_BACK,
    )(owners[0], d_image_got, full, patches, side, loss_sums)[0]
    outgoing, keep, send = lax.optimization_barrier((outgoing, keep, send))
    arrived = lax.all_to_all(outgoing, "fsdp", 0, 0, tiled=True)
    if ranks > 2:
        d_caption, *blocks = call(
            split_body,
            [(shape((slots, width), F32), vspec())] + [(shape((slots, width), BF16), vspec())] * 3,
            [vspec(), vspec()],
            40_000_000,
            1_000_000,
            name="split",
        )(keep, swapped(send, NEXT_BIT))
        blocks = [swapped(block, bit) for block, bit in zip(blocks, Z_BITS)]
    else:
        d_caption, blocks = keep, [swapped(send, CORE_BIT)]

    pooled_got = (
        got[:, :heads]
        .reshape(peers, heads, slots, cut)
        .transpose(1, 0, 2, 3)
        .reshape(heads, peers * slots, cut)
    )
    batch = ranks * peers * slots

    def last(*refs):
        last_body(*refs, texts=batch)

    row_grad, value_grad, probe_t, gain_grad, loss_part = call(
        last,
        [
            (shape((1, slots, rows, width), BF16), hspec()),
            (shape((1, cut, width), BF16), vspec()),
            (shape((heads, cut), BF16), vspec()),
            (shape((1, cut), BF16), vspec()),
            (shape((1, 1), F32), vspec()),
        ],
        [hspec(), vspec()],
        400_000_000,
        3_000_000,
        [pltpu.VMEM((peers, 16, width), BF16), dma((2,))],
        name="last",
    )(arrived, pooled_got)

    loss_part, blocks = lax.optimization_barrier((loss_part, blocks))
    text_grad = call(
        finish_body,
        [(shape((slots, width), BF16), vspec())],
        [vspec()] * (3 + len(blocks)),
        0,
        0,
        name="finish",
    )(d_caption, caption_unit, caption_inv, *blocks)[0]

    return (loss_part, row_grad, text_grad[None], value_grad, probe_t.T[None], gain_grad)


def solution(mesh):
    placed = (
        P(("dp", "fsdp"), None, None, None),
        P(("dp", "fsdp"), None),
        P(("dp", "fsdp"), None),
        P(("dp", "fsdp"), None, None),
        P(),
        P(),
        P("fsdp", None),
        P(),
        P(),
    )
    return jax.shard_map(
        local,
        mesh=mesh,
        in_specs=placed,
        out_specs=(
            P("dp", "fsdp"),
            P(("dp", "fsdp"), None, None, None),
            P(("dp", "fsdp"), None, None),
            P("dp", "fsdp", None),
            P("dp", "fsdp", None),
            P("dp", "fsdp"),
        ),
        check_vma=False,
    )
```
